1024 devices in a mesh: dia: 8 (over z_lo), sub: 32 (over y, z_hi, core), rad: 4 (over x).
Axes of the slice: x: 4, y: 4, z: 32 (z_hi: 4, z_lo: 8; z = z_hi * 8 + z_lo), core: 2. Of those that a mesh axis runs over, the one named last changes fastest.
Arguments:
- sensitivity_heat: float32 [16, 512, 8192], P('rad', 'sub', 'dia'), may hold values from -1.1 to 5.3
- stored_heat: float32 [16, 512, 8192], P('rad', 'sub', 'dia'), may hold values from -1 to 521
- friction_diagonal: float32 [16, 512, 8192], P('rad', 'sub', 'dia'), may hold values from 0.1 to 12
- stored_motions: bfloat16 [2, 3, 16, 512, 8192], P(None, None, 'rad', 'sub', 'dia'), may hold values from -5 to 5
- record_choice_table: int32 [16], P('dia'), may hold values from 0 to 1
Outputs:
- adj_temperature: float32 [16, 512, 8192], P('rad', 'sub', 'dia')
- adj_velocity: float32 [3, 16, 512, 8192], P(None, 'rad', 'sub', 'dia')
The draws below stay inside these ranges and needn't reach their ends.
All inputs are finite; a program needn't handle non-finite values.
Results may differ from the reference program's by a relative error of at most 0.0003.
Values sent between devices are 32-bit elements; how exact they have to be, the bound alone decides.
A program may use at most 64 MiB of HBM per device.

```python
import jax
import jax.numpy as jnp

NB = 512
NSNAP = 2
SWEEPS = 3
DEPTH_SHELLS = 16
SIDEWAYS_POINTS = 512
DIAMONDS = 16
LOOP_POINTS = 8192


def cycle_fraction():
    return (jnp.arange(LOOP_POINTS, dtype=jnp.float32) / LOOP_POINTS)[None, None, :]


def draw_sensitivity_heat(key, part):
    key = jax.random.fold_in(key, 11)
    shape = (DEPTH_SHELLS, SIDEWAYS_POINTS, LOOP_POINTS)
    position = cycle_fraction()
    rough = jnp.clip(jax.random.normal(key, shape, jnp.float32), -3.0, 3.0)
    ramp = 0.5 + position
    return ramp * (1.0 + 0.5 * rough)


def draw_stored_heat(key, part):
    key = jax.random.fold_in(key, 23)
    shape = (DEPTH_SHELLS, SIDEWAYS_POINTS, LOOP_POINTS)
    rough = jnp.clip(jax.random.normal(key, shape, jnp.float32), -3.0, 3.0)
    layer_pos = jnp.arange(DEPTH_SHELLS, dtype=jnp.float32)[:, None, None]
    across_pos = jnp.arange(SIDEWAYS_POINTS, dtype=jnp.float32)[None, :, None]
    cycle_pos = (jnp.arange(LOOP_POINTS, dtype=jnp.int32) % NB).astype(jnp.float32)[None, None, :]
    return 0.3 * rough + 0.5 * (layer_pos + across_pos + cycle_pos)


def draw_friction_diagonal(key, part):
    key = jax.random.fold_in(key, 37)
    shape = (DEPTH_SHELLS, SIDEWAYS_POINTS, LOOP_POINTS)
    spread = jax.random.uniform(key, shape, jnp.float32, 0.0, 1.0)
    level = 0.1 * jnp.exp(jnp.log(30.0) * cycle_fraction())
    return level * jnp.exp(jnp.log(4.0) * spread)


def plant(result, own_key, least, largest):
    place = [jax.random.randint(jax.random.fold_in(own_key, axis), (), 0, length) for axis, length in enumerate(result.shape)]
    main_axis = result.shape.index(max(result.shape))
    next_to = place[:main_axis] + [(place[main_axis] + 1) % result.shape[main_axis]] + place[main_axis + 1:]
    return result.at[tuple(place)].set(least).at[tuple(next_to)].set(largest)


def block_levels(rng, shape, shards, least, top_value):
    level, own = 1.0, jax.random.fold_in(rng, 6)
    for axis_at, blocks in shards:
        heights = jnp.exp(jax.random.uniform(jax.random.fold_in(own, axis_at), (blocks,), jnp.float32, least / len(shards), top_value / len(shards)))
        level = level * jnp.repeat(heights, shape[axis_at] // blocks).reshape([-1 if axis == axis_at else 1 for axis in range(len(shape))])
    return level


def noise(stream_key, dims, scale, most, split=(), held_as=jnp.bfloat16):
    array = jax.random.normal(stream_key, dims, jnp.float32) * scale
    if len(split) > 0:
        array = block_levels(stream_key, dims, split, -0.22, 0.18) * array
    return jnp.clip(array, min=-most, max=most).astype(held_as)


def setup_inputs(seed: int = 0) -> dict:
    streams_of = jax.random.split(jax.random.key(seed), 6)
    return {
        "sensitivity_heat": draw_sensitivity_heat(jax.random.fold_in(streams_of[5], 71), 0),
        "stored_heat": draw_stored_heat(jax.random.fold_in(streams_of[5], 71), 0),
        "friction_diagonal": draw_friction_diagonal(jax.random.fold_in(streams_of[5], 71), 0),
        "stored_motions": noise(streams_of[3], (NSNAP, 3, DEPTH_SHELLS, SIDEWAYS_POINTS, LOOP_POINTS), 1.0, 5.0, ((2, 4), (3, 32), (4, 8))),
        "record_choice_table": plant(jax.random.randint(streams_of[4], (DIAMONDS,), 0, NSNAP), jax.random.fold_in(streams_of[4], 1), 0, NSNAP - 1).astype(jnp.int32),
    }


def adjacent_slots(field):
    padded = jnp.pad(field, ((0, 0), (1, 1), (1, 1), (0, 0)))
    upper = (padded[:, 2:, 1:-1], padded[:, 1:-1, 2:], jnp.roll(field, -1, axis=3))
    lower = (padded[:, :-2, 1:-1], padded[:, 1:-1, :-2], jnp.roll(field, 1, axis=3))
    return upper, lower


def reference(sensitivity_heat, stored_heat, friction_diagonal, stored_motions, record_choice_table):
    column_dia = jnp.arange(LOOP_POINTS, dtype=jnp.int32) // NB
    chosen = record_choice_table[column_dia]
    motion_speed = jnp.zeros((3, DEPTH_SHELLS, SIDEWAYS_POINTS, LOOP_POINTS), jnp.float32)
    for snap in range(NSNAP):
        motion_speed = motion_speed + jnp.where((chosen == snap)[None, None, None, :], stored_motions[snap].astype(jnp.float32), 0.0)
    piled_quantities = jnp.concatenate([sensitivity_heat[None], motion_speed * sensitivity_heat[None], stored_heat[None]], 0)
    upper, lower = adjacent_slots(piled_quantities)
    laplace = upper[0][0] + lower[0][0] + upper[1][0] + lower[1][0] + upper[2][0] + lower[2][0] - 6.0 * sensitivity_heat
    flux = (upper[0][1] - lower[0][1]) + (upper[1][2] - lower[1][2]) + (upper[2][3] - lower[2][3])
    advected = sensitivity_heat + 0.25 * laplace + 0.125 * flux
    source = jnp.stack([-0.5 * sensitivity_heat * (upper[c][4] - lower[c][4]) for c in range(3)], 0)
    diagonal = 6.0 + friction_diagonal[None]
    velocity_adj = jnp.zeros_like(source)
    residual = source
    for sweep in range(SWEEPS):
        scaled = residual / diagonal
        upper, lower = adjacent_slots(scaled)
        beside_all = upper[0] + lower[0] + upper[1] + lower[1] + upper[2] + lower[2]
        image = diagonal * scaled - beside_all
        alpha = jnp.sum(residual * scaled) / jnp.sum(scaled * image)
        velocity_adj = velocity_adj + alpha * scaled
        residual = residual - alpha * image
    return advected + 4.0 * velocity_adj[0], velocity_adj
```

```python
import functools

import jax
import jax.numpy as jnp
from jax import lax
from jax.experimental import pallas as pl
from jax.experimental.pallas import tpu as pltpu
from jax.sharding import PartitionSpec as P

MESH = pl.DeviceIdType.MESH
H = 4
Y_COUNT, CORES = 4, 2
ALPHA_LOW, ALPHA_HIGH = 0.5, 62.0


def later(x, axis):
    return pltpu.roll(x, x.shape[axis] - 1, axis)


def earlier(x, axis):
    return pltpu.roll(x, 1, axis)


def places(sizes):
    n_dia, n_sub, n_rad, n_y, n_core = sizes
    n_zh = n_sub // (n_y * n_core)
    dia, sub, rad = lax.axis_index("dia"), lax.axis_index("sub"), lax.axis_index("rad")
    y, zh, core = sub // (n_zh * n_core), (sub // n_core) % n_zh, sub % n_core
    n_z = n_zh * n_dia
    n_g = n_rad * n_y * n_core
    z = zh * n_dia + dia
    g = (rad * n_y + y) * n_core + core

    def along_z(k):
        t = lax.rem(z + k, n_z)
        return {"sub": (y * n_zh + t // n_dia) * n_core + core, "dia": t % n_dia}

    def in_plane(k):
        t = lax.rem(g + k, n_g)
        r2, y2, c2 = t // (n_y * n_core), (t // n_core) % n_y, t % n_core
        return {"sub": (y2 * n_zh + zh) * n_core + c2, "rad": r2}

    return dia, sub, rad, core, z, g, n_z, n_g, along_z, in_plane


def kernel(
    sizes, table, s_hbm, t_hbm, f_hbm, m_hbm, temp_hbm, vel_hbm,
    s_v, d_v, m_v, T, Q, I, z0, z1, z2, eu0, ed0,
    sub_out, sub_in, dia_out, dia_in, mine, plane, column, temp_v, vel_v,
    load_sem, store_sem, dia_s, dia_r, rad_s, rad_r, sub_s, sub_r, cor_s, cor_r, fwd_s, fwd_r,
    plane_s, plane_r, column_s, column_r, relay,
):
    n_dia, n_sub, n_rad, n_y, n_core = sizes
    layers, rows, width = s_v.shape
    full_rows, full = rows + 8, width + 128
    dia, sub, rad, core, z, g, n_z, n_g, along_z, in_plane = places(sizes)
    reach = max(1, n_z // 4)
    own = pl.ds(H, layers)
    near = [k for k in range(1, n_z) if min(k, n_z - k) <= reach]

    has_up, has_down = sub < n_sub - 1, sub > 0
    has_above, has_below = rad < n_rad - 1, rad > 0
    above, below = {"rad": jnp.minimum(rad + 1, n_rad - 1)}, {"rad": jnp.maximum(rad - 1, 0)}
    up, down = {"sub": jnp.minimum(sub + 1, n_sub - 1)}, {"sub": jnp.maximum(sub - 1, 0)}
    right, left = {"dia": lax.rem(dia + 1, n_dia)}, {"dia": lax.rem(dia + n_dia - 1, n_dia)}

    barrier = pltpu.get_barrier_semaphore()
    for k in near:
        pl.semaphore_signal(barrier, inc=1, device_id=along_z(k), device_id_type=MESH)
    far_up = jnp.logical_and(core == n_core - 1, has_up)
    far_down = jnp.logical_and(core == 0, has_down)

    @pl.when(far_up)
    def _():
        pl.semaphore_signal(barrier, inc=1, device_id=up, device_id_type=MESH)

    @pl.when(far_down)
    def _():
        pl.semaphore_signal(barrier, inc=1, device_id=down, device_id_type=MESH)

    for k in range(1, n_g):
        pl.semaphore_signal(barrier, inc=1, device_id=in_plane(k), device_id_type=MESH)

    loads = [
        pltpu.make_async_copy(s_hbm, s_v, load_sem.at[0]),
        pltpu.make_async_copy(f_hbm, d_v, load_sem.at[1]),
        pltpu.make_async_copy(t_hbm, T.at[own, pl.ds(0, rows), pl.ds(0, width)], load_sem.at[2]),
        pltpu.make_async_copy(m_hbm, m_v, load_sem.at[3]),
    ]
    for copy in loads:
        copy.start()
    for copy in loads:
        copy.wait()

    lane = lax.broadcasted_iota(jnp.int32, (1, width), 1)
    picks = [table[i] for i in range(2)]
    choice = jnp.where(lane < width // 2, picks[0], picks[1])

    def motion(c, layer, row=slice(None)):
        return jnp.where(
            choice == 0,
            m_v[0, c, layer].astype(jnp.float32)[row],
            m_v[1, c, layer].astype(jnp.float32)[row],
        )

    def prepare(layer, carry):
        s = s_v[layer]
        diagonal = 6.0 + d_v[layer]
        d_v[layer] = diagonal
        inverse = 1.0 / diagonal
        I[H + layer, :rows, :width] = inverse
        Q[H + layer, :rows, :width] = -0.5 * s * inverse
        v = motion(0, layer)
        eu0[layer + 1] = (0.25 + 0.125 * v) * s
        ed0[layer + 1] = (0.25 - 0.125 * v) * s
        return carry

    lax.fori_loop(0, layers, prepare, 0)

    def pack(columns, edge):
        for l in range(layers):
            sub_out[0, l, 0:4, columns] = T[H + l, rows - 4 : rows, columns]
            sub_out[0, l, 4:7, columns] = Q[H + l, rows - 3 : rows, columns]
            sub_out[0, layers, 2 * l : 2 * l + 2, columns] = I[H + l, rows - 2 : rows, columns]
            sub_out[1, l, 0:4, columns] = T[H + l, 0:4, columns]
            sub_out[1, l, 4:7, columns] = Q[H + l, 0:3, columns]
            sub_out[1, layers, 2 * l : 2 * l + 2, columns] = I[H + l, 0:2, columns]
            if edge:
                v = motion(1, l)
                s = s_v[l]
                sub_out[0, l, 7:8, columns] = ((0.25 - 0.125 * v) * s)[rows - 1 : rows]
                sub_out[1, l, 7:8, columns] = ((0.25 + 0.125 * v) * s)[0:1]
            else:
                sub_out[0, l, 7:8, columns] = T[H + l, 0:1, columns]
                sub_out[1, l, 7:8, columns] = T[H + l, 0:1, columns]

    main, side = slice(0, width), slice(width, full)
    pack(main, True)

    tile_lane = lax.broadcasted_iota(jnp.int32, (1, 128), 1)
    packed = [jnp.zeros((8, 128), jnp.float32), jnp.zeros((8, 128), jnp.float32)]
    for l in range(layers):
        for half in range(rows // 8):
            k = l * (rows // 8) + half
            group = slice(8 * half, 8 * half + 8)
            for side_at, at in ((0, slice(width - 128, width)), (1, slice(0, 128))):
                pick = picks[1] if side_at == 0 else picks[0]
                v = jnp.where(
                    pick == 0,
                    m_v[0, 2, l, :, at].astype(jnp.float32)[group],
                    m_v[1, 2, l, :, at].astype(jnp.float32)[group],
                )
                sign = -0.125 if side_at == 0 else 0.125
                e = (0.25 + sign * v) * s_v[l, group, at]
                items = (T[H + l, group, at], Q[H + l, group, at], I[H + l, group, at], e)
                tile = packed[side_at]
                for n, item in enumerate(items):
                    if side_at == 0:
                        low = 124 - 4 * n - 16 * k
                        moved = pltpu.roll(item, (low - 124) % 128, 1)
                    else:
                        low = 4 * n + 16 * k
                        moved = pltpu.roll(item, low % 128, 1)
                    tile = jnp.where((tile_lane >= low) & (tile_lane < low + 4), moved, tile)
                packed[side_at] = tile
    dia_out[0] = packed[0]
    dia_out[1] = packed[1]

    halo_low, halo_high = pl.ds(0, H), pl.ds(H + layers, H)

    @pl.when(jnp.logical_not(has_below))
    def _():
        for ref in (T, Q, I):
            ref[halo_low] = jnp.zeros((H, full_rows, full), jnp.float32)
        ed0[0] = jnp.zeros((rows, width), jnp.float32)

    @pl.when(jnp.logical_not(has_above))
    def _():
        for ref in (T, Q, I):
            ref[halo_high] = jnp.zeros((H, full_rows, full), jnp.float32)
        eu0[layers + 1] = jnp.zeros((rows, width), jnp.float32)

    @pl.when(jnp.logical_not(has_down))
    def _():
        sub_in[0] = jnp.zeros(sub_in.shape[1:], jnp.float32)

    @pl.when(jnp.logical_not(has_up))
    def _():
        sub_in[1] = jnp.zeros(sub_in.shape[1:], jnp.float32)

    pl.semaphore_wait(
        barrier, len(near) + n_g - 1 + far_up.astype(jnp.int32) + far_down.astype(jnp.int32)
    )

    def send(src, dst, ssem, rsem, device):
        return pltpu.make_async_remote_copy(
            src_ref=src, dst_ref=dst, send_sem=ssem, recv_sem=rsem,
            device_id=device, device_id_type=MESH,
        )

    here, there = slice(0, width), slice(width, full)
    sub_main = [
        send(sub_out.at[i, :, :, pl.ds(0, width)], sub_in.at[i, :, :, pl.ds(0, width)], sub_s.at[i], sub_r.at[i], to)
        for i, to in enumerate((up, down))
    ]
    sub_side = [
        send(sub_out.at[i, :, :, pl.ds(width, 128)], sub_in.at[i, :, :, pl.ds(width, 128)], cor_s.at[i], cor_r.at[i], to)
        for i, to in enumerate((up, down))
    ]
    dia_copies = [
        send(dia_out.at[i], dia_in.at[i], dia_s.at[i], dia_r.at[i], to)
        for i, to in enumerate((right, left))
    ]

    def slab(ref, first, count, rows_at, lanes_at):
        return ref.at[pl.ds(first, count), pl.ds(*rows_at), pl.ds(*lanes_at)]

    def layer_copies(counts, rows_at, lanes_at, ssem, rsem):
        both = [[], []]
        for n, (ref, count) in enumerate(zip((T, Q, I), counts)):
            both[0].append(send(
                slab(ref, H + layers - count, count, rows_at, lanes_at),
                slab(ref, H - count, count, rows_at, lanes_at),
                ssem.at[0, n], rsem.at[0, n], above,
            ))
            both[1].append(send(
                slab(ref, H, count, rows_at, lanes_at),
                slab(ref, H + layers, count, rows_at, lanes_at),
                ssem.at[1, n], rsem.at[1, n], below,
            ))
        return both

    rad_main = layer_copies((4, 3, 2), (0, rows), (0, width), rad_s, rad_r)
    rad_main[0].append(send(ed0.at[layers], ed0.at[0], rad_s.at[0, 3], rad_r.at[0, 3], above))
    rad_main[1].append(send(eu0.at[1], eu0.at[layers + 1], rad_s.at[1, 3], rad_r.at[1, 3], below))
    rad_side = layer_copies((3, 2, 1), (0, rows), (width, 128), fwd_s.at[0], fwd_r.at[0])
    rad_rows = layer_copies((3, 2, 1), (rows, 8), (0, full), fwd_s.at[1], fwd_r.at[1])

    def start(copies, flag):
        @pl.when(flag)
        def _():
            for copy in copies:
                copy.start()

    def arrived(copies, flag):
        @pl.when(flag)
        def _():
            for copy in copies:
                copy.wait_recv()

    def left_here(copies, flag):
        @pl.when(flag)
        def _():
            for copy in copies:
                copy.wait_send()

    start([sub_main[0]], has_up)
    start([sub_main[1]], has_down)
    for copy in dia_copies:
        copy.start()
    start(rad_main[0], has_above)
    start(rad_main[1], has_below)

    for k in sorted({reach, n_z - reach}):
        pl.semaphore_signal(relay, inc=1, device_id=along_z(k), device_id_type=MESH)

    for copy in dia_copies:
        copy.wait_recv()
    eu2_side, ed2_side = [], []
    for l in range(layers):
        for half in range(rows // 8):
            k = l * (rows // 8) + half
            group = slice(8 * half, 8 * half + 8)
            for n, ref in enumerate((T, Q, I)):
                from_left = pltpu.roll(dia_in[0], (4 * n + 16 * k) % 128, 1)
                from_right = pltpu.roll(dia_in[1], (-4 * n - 16 * k) % 128, 1)
                ref[H + l, group, width:full] = jnp.where(tile_lane < 64, from_right, from_left)
    pack(side, False)
    start([sub_side[0]], has_up)
    start([sub_side[1]], has_down)
    start(rad_side[0], has_above)
    start(rad_side[1], has_below)

    def unpack(columns):
        for l in range(layers):
            T[H + l, rows + 4 : rows + 8, columns] = sub_in[0, l, 0:4, columns]
            Q[H + l, rows + 5 : rows + 8, columns] = sub_in[0, l, 4:7, columns]
            I[H + l, rows + 6 : rows + 8, columns] = sub_in[0, layers, 2 * l : 2 * l + 2, columns]
            T[H + l, rows : rows + 4, columns] = sub_in[1, l, 0:4, columns]
            Q[H + l, rows : rows + 3, columns] = sub_in[1, l, 4:7, columns]
            I[H + l, rows : rows + 2, columns] = sub_in[1, layers, 2 * l : 2 * l + 2, columns]

    arrived([sub_main[0]], has_down)
    arrived([sub_main[1]], has_up)
    unpack(main)
    arrived([sub_side[0]], has_down)
    arrived([sub_side[1]], has_up)
    unpack(side)
    start(rad_rows[0], has_above)
    start(rad_rows[1], has_below)
    for group in (rad_main, rad_side, rad_rows):
        arrived(group[0], has_below)
        arrived(group[1], has_above)

    def first(L, carry):
        t, q = T[L], Q[L]
        z0[0, L] = q * (T[L + 1] - T[L - 1])
        z0[1, L] = q * (later(t, 0) - earlier(t, 0))
        z0[2, L] = q * (later(t, 1) - earlier(t, 1))
        return carry

    lax.fori_loop(1, layers + 2 * H - 1, first, 0)

    def beside(ref, c, L):
        x = ref[c, L]
        rows_sum = later(x, 0) + earlier(x, 0)
        lanes_sum = later(x, 1) + earlier(x, 1)
        return ref[c, L + 1] + ref[c, L - 1] + rows_sum + lanes_sum

    def second(L, carry):
        for c in range(3):
            z1[c, L] = I[L] * beside(z0, c, L)
        return carry

    lax.fori_loop(2, layers + 2 * H - 2, second, 0)

    def third(L, carry):
        for c in range(3):
            z2[c, L] = I[L] * beside(z1, c, L)
        return carry

    lax.fori_loop(3, layers + 2 * H - 3, third, 0)

    def folded(x):
        total = jnp.zeros((8, 128), jnp.float32)
        for r in range(0, rows, 8):
            for w in range(0, width, 128):
                total = total + x[r : r + 8, w : w + 128]
        return total

    def moments(l, sums):
        L = H + l
        d = d_v[l]
        new = [0.0] * 6
        for c in range(3):
            a, b, e = z0[c, L, :rows, :width], z1[c, L, :rows, :width], z2[c, L, :rows, :width]
            y = beside(z2, c, L)[:rows, :width]
            da, db, de = d * a, d * b, d * e
            for j, term in enumerate((da * a, da * b, db * b, db * e, de * e, e * y)):
                new[j] = new[j] + term
        return tuple(total + folded(x) for total, x in zip(sums, new))

    sums = lax.fori_loop(0, layers, moments, (jnp.zeros((8, 128), jnp.float32),) * 6)

    row = jnp.zeros((1, 128), jnp.float32)
    for j in range(6):
        row = jnp.where(tile_lane == j, jnp.sum(sums[j], keepdims=True), row)

    def exchange(value, slots, count, index, peer, ssem, rsem, order):
        mine[...] = value
        slots[index] = value
        for k in order:
            send(mine, slots.at[index], ssem, rsem, peer(k)).start()
        return send(slots.at[pl.ds(0, count - 1)], slots.at[pl.ds(0, count - 1)], ssem, rsem, peer(1))

    copies = exchange(row, plane, n_g, g, in_plane, plane_s, plane_r, range(1, n_g))
    copies.wait_recv()
    copies.wait_send()
    row = jnp.sum(plane[...], axis=0)
    far_first = sorted(range(1, n_z), key=lambda k: -min(k, n_z - k))
    pl.semaphore_wait(relay, len({reach, n_z - reach}))
    copies = exchange(row, column, n_z, z, along_z, column_s, column_r, far_first)

    def advect(l, carry):
        s = s_v[l]
        v1, v2 = motion(1, l), motion(2, l)
        row_at = lax.broadcasted_iota(jnp.int32, (rows, width), 0)
        total = -0.5 * s + eu0[l + 2] + ed0[l]
        u, w = (0.25 + 0.125 * v1) * s, (0.25 - 0.125 * v1) * s
        total = total + jnp.where(row_at == rows - 1, sub_in[1, l, 7:8, :width], later(u, 0))
        total = total + jnp.where(row_at == 0, sub_in[0, l, 7:8, :width], earlier(w, 0))
        u, w = (0.25 + 0.125 * v2) * s, (0.25 - 0.125 * v2) * s
        temp_v[l] = total + later(u, 1) + earlier(w, 1)
        return carry

    lax.fori_loop(0, layers, advect, 0)
    for l in range(layers):
        for half in range(rows // 8):
            k = l * (rows // 8) + half
            group = slice(8 * half, 8 * half + 8)
            s_low, s_high = s_v[l, group, 0:128], s_v[l, group, width - 128 : width]

            def speed(at, pick, group=group, l=l):
                return jnp.where(
                    pick == 0,
                    m_v[0, 2, l, :, at].astype(jnp.float32)[group],
                    m_v[1, 2, l, :, at].astype(jnp.float32)[group],
                )

            low, high = slice(0, 128), slice(width - 128, width)
            u = pltpu.roll((0.25 + 0.125 * speed(low, picks[0])) * s_low, 127, 1)
            w = pltpu.roll((0.25 - 0.125 * speed(high, picks[1])) * s_high, 1, 1)
            from_left = pltpu.roll(dia_in[0], (13 + 16 * k) % 128, 1)
            from_right = pltpu.roll(dia_in[1], (127 - 12 - 16 * k) % 128, 1)
            temp_v[l, group, low] += jnp.where(tile_lane == 0, from_left - w, 0.0)
            temp_v[l, group, high] += jnp.where(tile_lane == 127, from_right - u, 0.0)

    copies.wait_recv()
    copies.wait_send()
    row = jnp.sum(column[...], axis=0)
    m0, m1, m2, m3, m4, m5 = (
        jnp.sum(jnp.where(tile_lane == j, row, 0.0), axis=1, keepdims=True) for j in range(6)
    )

    def step(p):
        a, b, c = p
        square = (a * a, 2.0 * a * b, b * b + 2.0 * a * c, 2.0 * b * c, c * c)
        energy = sum(x * m for x, m in zip(square, (m0, m1, m2, m3, m4)))
        moved = sum(x * m for x, m in zip(square, (m1, m2, m3, m4, m5)))
        return jnp.clip(energy / (energy - moved), ALPHA_LOW, ALPHA_HIGH)

    one, none = jnp.ones_like(m0), jnp.zeros_like(m0)
    p0 = (one, none, none)
    alpha0 = step(p0)
    p1 = (1.0 - alpha0, alpha0, none)
    alpha1 = step(p1)
    p2 = (p1[0] * (1.0 - alpha1), p1[1] * (1.0 - alpha1) + p1[0] * alpha1, p1[1] * alpha1)
    alpha2 = step(p2)
    c0, c1, c2 = (alpha0 * x + alpha1 * y + alpha2 * w for x, y, w in zip(p0, p1, p2))

    stores = []
    for l in range(layers):
        stores.append(pltpu.make_async_copy(vel_v.at[:, l], vel_hbm.at[:, l], store_sem.at[0, l]))
        stores.append(pltpu.make_async_copy(temp_v.at[l], temp_hbm.at[l], store_sem.at[1, l]))
        for c in range(3):
            at = (c, H + l, slice(0, rows), slice(0, width))
            velocity = c0 * z0[at] + c1 * z1[at] + c2 * z2[at]
            vel_v[c, l] = velocity
            if c == 0:
                temp_v[l] = temp_v[l] + 4.0 * velocity
        stores[-2].start()
        stores[-1].start()

    left_here([sub_main[0], sub_side[0]], has_up)
    left_here([sub_main[1], sub_side[1]], has_down)
    for copy in dia_copies:
        copy.wait_send()
    for group in (rad_main, rad_side, rad_rows):
        left_here(group[0], has_above)
        left_here(group[1], has_below)
    for copy in stores:
        copy.wait()


def solution(mesh):
    shape = mesh.shape
    n_y = Y_COUNT if shape["sub"] >= 32 else 1
    sizes = (shape["dia"], shape["sub"], shape["rad"], n_y, CORES)
    n_z = shape["dia"] * shape["sub"] // (n_y * CORES)
    n_g = shape["rad"] * n_y * CORES

    def shards(sensitivity_heat, stored_heat, friction_diagonal, stored_motions, record_choice_table):
        layers, rows, width = sensitivity_heat.shape
        tall, wide, long = layers + 2 * H, rows + 8, width + 128
        f32 = jnp.float32
        block = pltpu.VMEM((layers, rows, width), f32)
        field = pltpu.VMEM((tall, wide, long), f32)
        vector = pltpu.VMEM((3, tall, wide, long), f32)
        dma = pltpu.SemaphoreType.DMA
        anywhere = pl.BlockSpec(memory_space=pl.ANY)
        return pl.pallas_call(
            functools.partial(kernel, sizes),
            out_shape=(
                jax.ShapeDtypeStruct((layers, rows, width), f32),
                jax.ShapeDtypeStruct((3, layers, rows, width), f32),
            ),
            in_specs=[pl.BlockSpec(memory_space=pltpu.SMEM)] + [anywhere] * 4,
            out_specs=(anywhere, anywhere),
            scratch_shapes=[
                block, block, pltpu.VMEM(stored_motions.shape, stored_motions.dtype),
                field, field, field, vector, vector, vector,
                pltpu.VMEM((layers + 2, rows, width), f32), pltpu.VMEM((layers + 2, rows, width), f32),
                pltpu.VMEM((2, layers + 1, 8, long), f32), pltpu.VMEM((2, layers + 1, 8, long), f32),
                pltpu.VMEM((2, 8, 128), f32), pltpu.VMEM((2, 8, 128), f32),
                pltpu.VMEM((1, 128), f32), pltpu.VMEM((n_g, 1, 128), f32), pltpu.VMEM((n_z, 1, 128), f32),
                block, pltpu.VMEM((3, layers, rows, width), f32),
                dma((4,)), dma((2, layers)), dma((2,)), dma((2,)), dma((2, 4)), dma((2, 4)),
                dma((2,)), dma((2,)), dma((2,)), dma((2,)), dma((2, 2, 3)), dma((2, 2, 3)),
                dma, dma, dma, dma, pltpu.SemaphoreType.REGULAR,
            ],
            compiler_params=pltpu.CompilerParams(
                collective_id=0, has_side_effects=True, vmem_limit_bytes=48 * 2**20
            ),
            name="adjoint_step",
        )(record_choice_table, sensitivity_heat, stored_heat, friction_diagonal, stored_motions)

    placed = (
        P("rad", "sub", "dia"),
        P("rad", "sub", "dia"),
        P("rad", "sub", "dia"),
        P(None, None, "rad", "sub", "dia"),
        P("dia"),
    )
    return jax.shard_map(
        shards,
        mesh=mesh,
        in_specs=placed,
        out_specs=(P("rad", "sub", "dia"), P(None, "rad", "sub", "dia")),
        check_vma=False,
    )
```

```python
import functools

import jax
import jax.numpy as jnp
from jax import lax
from jax.experimental import pallas as pl
from jax.experimental.pallas import tpu as pltpu
from jax.sharding import PartitionSpec as P

MESH = pl.DeviceIdType.MESH
H = 4
Y_COUNT, CORES = 4, 2
ALPHA_LOW, ALPHA_HIGH = 0.5, 62.0


def later(x, axis):
    return pltpu.roll(x, x.shape[axis] - 1, axis)


def earlier(x, axis):
    return pltpu.roll(x, 1, axis)


def places(sizes):
    n_dia, n_sub, n_rad, n_y, n_core = sizes
    n_zh = n_sub // (n_y * n_core)
    dia, sub, rad = lax.axis_index("dia"), lax.axis_index("sub"), lax.axis_index("rad")
    y, zh, core = sub // (n_zh * n_core), (sub // n_core) % n_zh, sub % n_core
    n_z = n_zh * n_dia
    n_g = n_rad * n_y * n_core
    z = zh * n_dia + dia
    g = (rad * n_y + y) * n_core + core

    def along_z(k):
        t = lax.rem(z + k, n_z)
        return {"sub": (y * n_zh + t // n_dia) * n_core + core, "dia": t % n_dia}

    def in_plane(k):
        t = lax.rem(g + k, n_g)
        r2, y2, c2 = t // (n_y * n_core), (t // n_core) % n_y, t % n_core
        return {"sub": (y2 * n_zh + zh) * n_core + c2, "rad": r2}

    return dia, sub, rad, core, z, g, n_z, n_g, along_z, in_plane


def kernel(
    sizes, table, s_hbm, t_hbm, f_hbm, m_hbm, adv_hbm, zs_hbm, coef_ref,
    s_v, d_v, m_v, T, Q, I, z0, z1, z2, eu0, ed0,
    sub_out, sub_in, dia_out, dia_in, fwd_out, fwd_in, mine, plane, column, temp_v,
    load_sem, store_sem, dia_s, dia_r, rad_s, rad_r, sub_s, sub_r, cor_s, cor_r, fwd_s, fwd_r, late_s, late_r, edge_s, edge_r,
    plane_s, plane_r, column_s, column_r, relay,
):
    n_dia, n_sub, n_rad, n_y, n_core = sizes
    layers, rows, width = s_v.shape
    full_rows, full = rows + 8, width + 128
    dia, sub, rad, core, z, g, n_z, n_g, along_z, in_plane = places(sizes)
    reach = max(1, n_z // 4)
    own = pl.ds(H, layers)
    near = sorted((k for k in range(1, n_z) if min(k, n_z - k) <= reach), key=lambda k: -min(k, n_z - k))

    has_up, has_down = sub < n_sub - 1, sub > 0
    has_above, has_below = rad < n_rad - 1, rad > 0
    above, below = {"rad": jnp.minimum(rad + 1, n_rad - 1)}, {"rad": jnp.maximum(rad - 1, 0)}
    up, down = {"sub": jnp.minimum(sub + 1, n_sub - 1)}, {"sub": jnp.maximum(sub - 1, 0)}
    right, left = {"dia": lax.rem(dia + 1, n_dia)}, {"dia": lax.rem(dia + n_dia - 1, n_dia)}

    barrier = pltpu.get_barrier_semaphore()
    far_up = jnp.logical_and(core == n_core - 1, has_up)
    far_down = jnp.logical_and(core == 0, has_down)

    @pl.when(far_up)
    def _():
        pl.semaphore_signal(barrier, inc=1, device_id=up, device_id_type=MESH)

    @pl.when(far_down)
    def _():
        pl.semaphore_signal(barrier, inc=1, device_id=down, device_id_type=MESH)

    for k in near:
        pl.semaphore_signal(barrier, inc=1, device_id=along_z(k), device_id_type=MESH)

    loads = [
        pltpu.make_async_copy(s_hbm, s_v, load_sem.at[0]),
        pltpu.make_async_copy(f_hbm, d_v, load_sem.at[1]),
        pltpu.make_async_copy(t_hbm, T.at[own, pl.ds(0, rows), pl.ds(0, width)], load_sem.at[2]),
        pltpu.make_async_copy(m_hbm, m_v, load_sem.at[3]),
    ]
    for copy in loads:
        copy.start()
    for k in range(1, n_g):
        pl.semaphore_signal(barrier, inc=1, device_id=in_plane(k), device_id_type=MESH)
    for copy in loads:
        copy.wait()

    lane = lax.broadcasted_iota(jnp.int32, (1, width), 1)
    picks = [table[i] for i in range(2)]
    choice = jnp.where(lane < width // 2, picks[0], picks[1])

    def motion(c, layer, row=slice(None)):
        return jnp.where(
            choice == 0,
            m_v[0, c, layer].astype(jnp.float32)[row],
            m_v[1, c, layer].astype(jnp.float32)[row],
        )

    def prepare(layer, carry):
        s = s_v[layer]
        diagonal = 6.0 + d_v[layer]
        d_v[layer] = diagonal
        inverse = 1.0 / diagonal
        I[H + layer, :rows, :width] = inverse
        Q[H + layer, :rows, :width] = -0.5 * s * inverse
        v = motion(0, layer)
        eu0[layer + 1] = (0.25 + 0.125 * v) * s
        ed0[layer + 1] = (0.25 - 0.125 * v) * s
        return carry

    lax.fori_loop(0, layers, prepare, 0)

    def row_plan(way):
        if way == 0:
            t, q, i = (rows - 3, rows + 5, 3), (rows - 2, rows + 6, 2), (rows - 1, rows + 7, 1)
            deep = ((T, rows - 4, rows + 4), (Q, rows - 3, rows + 5), (I, rows - 2, rows + 6))
            deeper = range(layers // 2, layers)
        else:
            t, q, i = (0, rows, 3), (0, rows, 2), (0, rows, 1)
            deep = ((T, 3, rows + 3), (Q, 2, rows + 2), (I, 1, rows + 1))
            deeper = range(layers // 2)
        plan = []
        for pair in range(layers // 2):
            plan += [(T, 2 * pair, *t), (T, 2 * pair + 1, *t), (Q, 2 * pair, *q)]
        for pair in range(layers // 2):
            plan.append((Q, 2 * pair + 1, *q))
        plan += [(I, l, *i) for l in range(layers)]
        for l in deeper:
            plan += [(ref, l, src, dst, 1) for ref, src, dst in deep]
        at, placed = 0, []
        for ref, l, src, dst, count in plan:
            placed.append((ref, H + l, src, dst, count, at // 8, at % 8))
            at += count
        return placed

    def pack(columns):
        for way in range(2):
            for ref, L, src, _, count, tile, at in row_plan(way):
                sub_out[way, tile, at : at + count, columns] = ref[L, src : src + count, columns]

    def pack_edges():
        for l in range(layers):
            v = motion(1, l)
            s = s_v[l]
            sub_out[0, layers, l : l + 1, :width] = ((0.25 - 0.125 * v) * s)[rows - 1 : rows]
            sub_out[1, layers, l : l + 1, :width] = ((0.25 + 0.125 * v) * s)[0:1]

    main, side = slice(0, width), slice(width, full)
    pack(main)
    pack_edges()

    tile_lane = lax.broadcasted_iota(jnp.int32, (1, 128), 1)
    packed = [jnp.zeros((8, 128), jnp.float32), jnp.zeros((8, 128), jnp.float32)]
    for l in range(layers):
        for half in range(rows // 8):
            k = l * (rows // 8) + half
            group = slice(8 * half, 8 * half + 8)
            for side_at, at in ((0, slice(width - 128, width)), (1, slice(0, 128))):
                pick = picks[1] if side_at == 0 else picks[0]
                v = jnp.where(
                    pick == 0,
                    m_v[0, 2, l, :, at].astype(jnp.float32)[group],
                    m_v[1, 2, l, :, at].astype(jnp.float32)[group],
                )
                sign = -0.125 if side_at == 0 else 0.125
                e = (0.25 + sign * v) * s_v[l, group, at]
                items = (T[H + l, group, at], Q[H + l, group, at], I[H + l, group, at], e)
                tile = packed[side_at]
                for n, item in enumerate(items):
                    if side_at == 0:
                        low = 124 - 4 * n - 16 * k
                        moved = pltpu.roll(item, (low - 124) % 128, 1)
                    else:
                        low = 4 * n + 16 * k
                        moved = pltpu.roll(item, low % 128, 1)
                    tile = jnp.where((tile_lane >= low) & (tile_lane < low + 4), moved, tile)
                packed[side_at] = tile
    dia_out[0] = packed[0]
    dia_out[1] = packed[1]

    halo_low, halo_high = pl.ds(0, H), pl.ds(H + layers, H)

    @pl.when(jnp.logical_not(has_below))
    def _():
        fwd_in[0] = jnp.zeros(fwd_in.shape[1:], jnp.float32)
        for ref in (T, Q, I):
            ref[halo_low] = jnp.zeros((H, full_rows, full), jnp.float32)
        ed0[0] = jnp.zeros((rows, width), jnp.float32)

    @pl.when(jnp.logical_not(has_above))
    def _():
        fwd_in[1] = jnp.zeros(fwd_in.shape[1:], jnp.float32)
        for ref in (T, Q, I):
            ref[halo_high] = jnp.zeros((H, full_rows, full), jnp.float32)
        eu0[layers + 1] = jnp.zeros((rows, width), jnp.float32)

    @pl.when(jnp.logical_not(has_down))
    def _():
        sub_in[0] = jnp.zeros(sub_in.shape[1:], jnp.float32)

    @pl.when(jnp.logical_not(has_up))
    def _():
        sub_in[1] = jnp.zeros(sub_in.shape[1:], jnp.float32)

    pl.semaphore_wait(
        barrier, len(near) + n_g - 1 + far_up.astype(jnp.int32) + far_down.astype(jnp.int32)
    )

    def send(src, dst, ssem, rsem, device):
        return pltpu.make_async_remote_copy(
            src_ref=src, dst_ref=dst, send_sem=ssem, recv_sem=rsem,
            device_id=device, device_id_type=MESH,
        )

    sub_main = [
        send(sub_out.at[i, pl.ds(0, layers), :, pl.ds(0, width)], sub_in.at[i, pl.ds(0, layers), :, pl.ds(0, width)], sub_s.at[i], sub_r.at[i], to)
        for i, to in enumerate((up, down))
    ]
    sub_side = [
        send(sub_out.at[i, pl.ds(0, layers), :, pl.ds(width, 128)], sub_in.at[i, pl.ds(0, layers), :, pl.ds(width, 128)], cor_s.at[i], cor_r.at[i], to)
        for i, to in enumerate((up, down))
    ]
    sub_edge = [
        send(sub_out.at[i, layers, :, pl.ds(0, width)], sub_in.at[i, layers, :, pl.ds(0, width)], edge_s.at[i], edge_r.at[i], to)
        for i, to in enumerate((up, down))
    ]
    dia_copies = [
        send(dia_out.at[i], dia_in.at[i], dia_s.at[i], dia_r.at[i], to)
        for i, to in enumerate((right, left))
    ]

    def slab(ref, first, count, rows_at, lanes_at):
        return ref.at[pl.ds(first, count), pl.ds(*rows_at), pl.ds(*lanes_at)]

    def layer_copies(counts, rows_at, lanes_at, ssem, rsem, ahead=0):
        both = [[], []]
        for n, (ref, count) in enumerate(zip((T, Q, I), counts)):
            skip = (3 - n) if ahead else 0
            both[0].append(send(
                slab(ref, H + layers - count - skip, count, rows_at[0], lanes_at),
                slab(ref, H - count - skip, count, rows_at[0], lanes_at),
                ssem.at[0, n], rsem.at[0, n], above,
            ))
            both[1].append(send(
                slab(ref, H + skip, count, rows_at[1], lanes_at),
                slab(ref, H + layers + skip, count, rows_at[1], lanes_at),
                ssem.at[1, n], rsem.at[1, n], below,
            ))
        return both

    all_rows = ((0, rows), (0, rows))
    rad_main = layer_copies((3, 2, 1), all_rows, (0, width), rad_s.at[0], rad_r.at[0])
    rad_deep = layer_copies((1, 1, 1), ((8, 8), (0, 8)), (0, width), rad_s.at[1], rad_r.at[1], 1)
    rad_side = layer_copies((3, 2, 1), all_rows, (width, 128), fwd_s, fwd_r)
    rad_edge = [
        [send(ed0.at[layers], ed0.at[0], edge_s.at[2], edge_r.at[2], above)],
        [send(eu0.at[1], eu0.at[layers + 1], edge_s.at[3], edge_r.at[3], below)],
    ]
    rad_rows = [
        [send(fwd_out.at[i], fwd_in.at[i], late_s.at[i], late_r.at[i], to)]
        for i, to in enumerate((above, below))
    ]

    def corner_plan(way):
        far = (rows, 1) if way == 0 else (rows + 7, -1)
        near_side = (rows + 7, -1) if way == 0 else (rows, 1)

        def run(side, depth):
            return (side[0] if side[1] > 0 else side[0] - depth + 1, depth)

        plan = [(T, 1, *run(far, 3)), (T, 2, *run(far, 2)), (Q, 1, *run(far, 2)), (T, 3, *run(far, 1))]
        plan += [(T, 1, *run(near_side, 2)), (Q, 2, *run(far, 1)), (I, 1, *run(far, 1))]
        plan += [(T, 2, *run(near_side, 1)), (Q, 1, *run(near_side, 1))]
        at, placed = 0, []
        for ref, depth, first_row, count in plan:
            src = H + layers - depth if way == 0 else H + depth - 1
            dst = H - depth if way == 0 else H + layers + depth - 1
            placed.append((ref, src, dst, first_row, count, at // 8, at % 8))
            at += count
        return placed

    def start(copies, flag):
        @pl.when(flag)
        def _():
            for copy in copies:
                copy.start()

    def arrived(copies, flag):
        @pl.when(flag)
        def _():
            for copy in copies:
                copy.wait_recv()

    def left_here(copies, flag):
        @pl.when(flag)
        def _():
            for copy in copies:
                copy.wait_send()

    start([sub_main[0]], has_up)
    start([sub_main[1]], has_down)
    for copy in dia_copies:
        copy.start()
    for group in (rad_main, rad_deep):
        start(group[0], has_above)
        start(group[1], has_below)

    for k in sorted({reach, n_z - reach}):
        pl.semaphore_signal(relay, inc=1, device_id=along_z(k), device_id_type=MESH)

    for copy in dia_copies:
        copy.wait_recv()
    for l in range(layers):
        for half in range(rows // 8):
            k = l * (rows // 8) + half
            group = slice(8 * half, 8 * half + 8)
            for n, ref in enumerate((T, Q, I)):
                from_left = pltpu.roll(dia_in[0], (4 * n + 16 * k) % 128, 1)
                from_right = pltpu.roll(dia_in[1], (-4 * n - 16 * k) % 128, 1)
                ref[H + l, group, width:full] = jnp.where(tile_lane < 64, from_right, from_left)
    pack(side)
    start([sub_side[0]], has_up)
    start([sub_side[1]], has_down)
    start(rad_side[0], has_above)
    start(rad_side[1], has_below)
    start([sub_edge[0]], has_up)
    start([sub_edge[1]], has_down)
    start(rad_edge[0], has_above)
    start(rad_edge[1], has_below)

    def unpack(columns):
        for way in range(2):
            for ref, L, _, dst, count, tile, at in row_plan(way):
                ref[L, dst : dst + count, columns] = sub_in[way, tile, at : at + count, columns]

    arrived([sub_main[0]], has_down)
    arrived([sub_main[1]], has_up)
    unpack(main)
    arrived([sub_side[0]], has_down)
    arrived([sub_side[1]], has_up)
    unpack(side)
    for way in range(2):
        for ref, src, _, row_at, count, tile, at in corner_plan(way):
            fwd_out[way, tile, at : at + count] = ref[src, row_at : row_at + count]
    start(rad_rows[0], has_above)
    start(rad_rows[1], has_below)
    for group in (rad_main, rad_deep, rad_side, rad_rows):
        arrived(group[0], has_below)
        arrived(group[1], has_above)
    for way in range(2):
        for ref, _, dst, row_at, count, tile, at in corner_plan(way):
            ref[dst, row_at : row_at + count] = fwd_in[way, tile, at : at + count]

    low_half, high_half, every = slice(0, 8), slice(8, 16), slice(0, full_rows)
    bottom, top = H - 1, H + layers

    def first_at(L, at):
        t, q = T[L], Q[L, at]
        z0[0, L, at] = q * (T[L + 1, at] - T[L - 1, at])
        z0[1, L, at] = q * (later(t, 0) - earlier(t, 0))[at]
        z0[2, L, at] = q * (later(t[at], 1) - earlier(t[at], 1))

    def beside(ref, c, L, at):
        x = ref[c, L]
        rows_sum = (later(x, 0) + earlier(x, 0))[at]
        lanes_sum = later(x[at], 1) + earlier(x[at], 1)
        return ref[c, L + 1, at] + ref[c, L - 1, at] + rows_sum + lanes_sum

    def next_at(source, target, L, at):
        for c in range(3):
            target[c, L, at] = I[L, at] * beside(source, c, L, at)

    def over_layers(step, beyond):
        lax.fori_loop(bottom - beyond + 1, top + beyond, lambda L, carry: (step(L, every), carry)[1], 0)
        step(bottom - beyond, high_half)
        step(top + beyond, low_half)

    over_layers(first_at, 2)
    over_layers(lambda L, at: next_at(z0, z1, L, at), 1)
    over_layers(lambda L, at: next_at(z1, z2, L, at), 0)

    def folded(x):
        total = jnp.zeros((8, 128), jnp.float32)
        for r in range(0, rows, 8):
            for w in range(0, width, 128):
                total = total + x[r : r + 8, w : w + 128]
        return total

    row_at = lax.broadcasted_iota(jnp.int32, (rows, width), 0)

    def moments(l, sums):
        L = H + l
        d = d_v[l]
        new = [0.0] * 6
        for c in range(3):
            a, b, e = z0[c, L, :rows, :width], z1[c, L, :rows, :width], z2[c, L, :rows, :width]
            x = z2[c, L]
            ahead = jnp.where((row_at < 8) | (l < layers - 1), z2[c, L + 1, :rows, :width], 0.0)
            ahead += jnp.where((row_at < rows - 1) | (l < layers // 2), later(x, 0)[:rows, :width], 0.0)
            ahead += jnp.where((row_at == 0) & (l >= layers // 2), earlier(x, 0)[:rows, :width], 0.0)
            ahead += later(x[:rows], 1)[:, :width]
            da, db, de = d * a, d * b, d * e
            for j, term in enumerate((da * a, da * b, db * b, db * e, de * e, e * ahead)):
                new[j] = new[j] + term
        return tuple(total + folded(x) for total, x in zip(sums, new))

    sums = list(lax.fori_loop(0, layers, moments, (jnp.zeros((8, 128), jnp.float32),) * 6))
    for c in range(3):
        joint = z2[c, H, high_half, :width] * z2[c, bottom, high_half, :width]
        for w in range(0, width, 128):
            sums[5] = sums[5] + joint[:, w : w + 128]
    sums[5] = 2.0 * sums[5]

    row = jnp.zeros((1, 128), jnp.float32)
    for j in range(6):
        row = jnp.where(tile_lane == j, jnp.sum(sums[j], keepdims=True), row)

    def exchange(value, slots, count, index, peer, ssem, rsem, order):
        mine[...] = value
        slots[index] = value
        for k in order:
            send(mine, slots.at[index], ssem, rsem, peer(k)).start()
        return send(slots.at[pl.ds(0, count - 1)], slots.at[pl.ds(0, count - 1)], ssem, rsem, peer(1))

    copies = exchange(row, plane, n_g, g, in_plane, plane_s, plane_r, range(1, n_g))
    stores = [
        pltpu.make_async_copy(ref.at[:, own, pl.ds(0, rows), pl.ds(0, width)], zs_hbm.at[k], store_sem.at[k])
        for k, ref in enumerate((z0, z1, z2))
    ]
    copies.wait_recv()
    copies.wait_send()
    row = jnp.sum(plane[...], axis=0)
    far_first = sorted(range(1, n_z), key=lambda k: -min(k, n_z - k))
    pl.semaphore_wait(relay, len({reach, n_z - reach}))
    copies = exchange(row, column, n_z, z, along_z, column_s, column_r, far_first)

    for copy in stores:
        copy.start()
    arrived([sub_edge[0]], has_down)
    arrived([sub_edge[1]], has_up)
    arrived(rad_edge[0], has_below)
    arrived(rad_edge[1], has_above)

    def advect(l, carry):
        s = s_v[l]
        v1, v2 = motion(1, l), motion(2, l)
        total = -0.5 * s + eu0[l + 2] + ed0[l]
        u, w = (0.25 + 0.125 * v1) * s, (0.25 - 0.125 * v1) * s
        total = total + jnp.where(row_at == rows - 1, sub_in[1, layers, pl.ds(l, 1), :width], later(u, 0))
        total = total + jnp.where(row_at == 0, sub_in[0, layers, pl.ds(l, 1), :width], earlier(w, 0))
        u, w = (0.25 + 0.125 * v2) * s, (0.25 - 0.125 * v2) * s
        temp_v[l] = total + later(u, 1) + earlier(w, 1)
        return carry

    lax.fori_loop(0, layers, advect, 0)
    for l in range(layers):
        for half in range(rows // 8):
            k = l * (rows // 8) + half
            group = slice(8 * half, 8 * half + 8)
            s_low, s_high = s_v[l, group, 0:128], s_v[l, group, width - 128 : width]

            def speed(at, pick, group=group, l=l):
                return jnp.where(
                    pick == 0,
                    m_v[0, 2, l, :, at].astype(jnp.float32)[group],
                    m_v[1, 2, l, :, at].astype(jnp.float32)[group],
                )

            low, high = slice(0, 128), slice(width - 128, width)
            u = pltpu.roll((0.25 + 0.125 * speed(low, picks[0])) * s_low, 127, 1)
            w = pltpu.roll((0.25 - 0.125 * speed(high, picks[1])) * s_high, 1, 1)
            from_left = pltpu.roll(dia_in[0], (13 + 16 * k) % 128, 1)
            from_right = pltpu.roll(dia_in[1], (127 - 12 - 16 * k) % 128, 1)
            temp_v[l, group, low] += jnp.where(tile_lane == 0, from_left - w, 0.0)
            temp_v[l, group, high] += jnp.where(tile_lane == 127, from_right - u, 0.0)

    stores.append(pltpu.make_async_copy(temp_v, adv_hbm, store_sem.at[3]))
    stores[3].start()
    left_here([sub_main[0], sub_side[0], sub_edge[0]], has_up)
    left_here([sub_main[1], sub_side[1], sub_edge[1]], has_down)
    for copy in dia_copies:
        copy.wait_send()
    for group in (rad_main, rad_deep, rad_side, rad_rows, rad_edge):
        left_here(group[0], has_above)
        left_here(group[1], has_below)
    for copy in stores:
        copy.wait()

    copies.wait_recv()
    copies.wait_send()
    row = jnp.sum(column[...], axis=0)
    m0, m1, m2, m3, m4, m5 = (
        jnp.sum(jnp.where(tile_lane == j, row, 0.0), axis=1, keepdims=True) for j in range(6)
    )

    def step(p):
        a, b, c = p
        square = (a * a, 2.0 * a * b, b * b + 2.0 * a * c, 2.0 * b * c, c * c)
        energy = sum(x * m for x, m in zip(square, (m0, m1, m2, m3, m4)))
        moved = sum(x * m for x, m in zip(square, (m1, m2, m3, m4, m5)))
        return jnp.clip(energy / (energy - moved), ALPHA_LOW, ALPHA_HIGH)

    one, none = jnp.ones_like(m0), jnp.zeros_like(m0)
    p0 = (one, none, none)
    alpha0 = step(p0)
    p1 = (1.0 - alpha0, alpha0, none)
    alpha1 = step(p1)
    p2 = (p1[0] * (1.0 - alpha1), p1[1] * (1.0 - alpha1) + p1[0] * alpha1, p1[1] * alpha1)
    alpha2 = step(p2)
    c0, c1, c2 = (alpha0 * x + alpha1 * y + alpha2 * w for x, y, w in zip(p0, p1, p2))

    wide = jnp.zeros((8, 128), jnp.float32)
    row_of = lax.broadcasted_iota(jnp.int32, (8, 128), 0)
    for n, value in enumerate((c0, c1, c2)):
        wide = jnp.where(row_of == n, value, wide)
    coef_ref[...] = wide


def finish(coef_ref, adv_ref, zs_ref, temp_ref, vel_ref):
    c0, c1, c2 = (coef_ref[n : n + 1, 0:1] for n in range(3))
    for c in range(3):
        velocity = c0 * zs_ref[0, c, 0] + c1 * zs_ref[1, c, 0] + c2 * zs_ref[2, c, 0]
        vel_ref[c, 0] = velocity
        if c == 0:
            temp_ref[0] = adv_ref[0] + 4.0 * velocity


def solution(mesh):
    shape = mesh.shape
    n_y = Y_COUNT if shape["sub"] >= 32 else 1
    sizes = (shape["dia"], shape["sub"], shape["rad"], n_y, CORES)
    n_z = shape["dia"] * shape["sub"] // (n_y * CORES)
    n_g = shape["rad"] * n_y * CORES

    def shards(sensitivity_heat, stored_heat, friction_diagonal, stored_motions, record_choice_table):
        layers, rows, width = sensitivity_heat.shape
        tall, wide, long = layers + 2 * H, rows + 8, width + 128
        f32 = jnp.float32
        block = pltpu.VMEM((layers, rows, width), f32)
        field = pltpu.VMEM((tall, wide, long), f32)
        vector = pltpu.VMEM((3, tall, wide, long), f32)
        dma = pltpu.SemaphoreType.DMA
        in_hbm = pl.BlockSpec(memory_space=pltpu.HBM)
        advected, zs, coefficients = pl.pallas_call(
            functools.partial(kernel, sizes),
            out_shape=(
                jax.ShapeDtypeStruct((layers, rows, width), f32),
                jax.ShapeDtypeStruct((3, 3, layers, rows, width), f32),
                jax.ShapeDtypeStruct((8, 128), f32),
            ),
            in_specs=[pl.BlockSpec(memory_space=pltpu.SMEM)] + [in_hbm] * 4,
            out_specs=(in_hbm, in_hbm, pl.BlockSpec(memory_space=pltpu.VMEM)),
            scratch_shapes=[
                block, block, pltpu.VMEM(stored_motions.shape, stored_motions.dtype),
                field, field, field, vector, vector, vector,
                pltpu.VMEM((layers + 2, rows, width), f32), pltpu.VMEM((layers + 2, rows, width), f32),
                pltpu.VMEM((2, layers + 1, 8, long), f32), pltpu.VMEM((2, layers + 1, 8, long), f32),
                pltpu.VMEM((2, 8, 128), f32), pltpu.VMEM((2, 8, 128), f32),
                pltpu.VMEM((2, 2, 8, long), f32), pltpu.VMEM((2, 2, 8, long), f32),
                pltpu.VMEM((1, 128), f32), pltpu.VMEM((n_g, 1, 128), f32), pltpu.VMEM((n_z, 1, 128), f32),
                block,
                dma((4,)), dma((4,)), dma((2,)), dma((2,)), dma((2, 2, 3)), dma((2, 2, 3)),
                dma((2,)), dma((2,)), dma((2,)), dma((2,)), dma((2, 3)), dma((2, 3)),
                dma((2,)), dma((2,)), dma((4,)), dma((4,)),
                dma, dma, dma, dma, pltpu.SemaphoreType.REGULAR,
            ],
            compiler_params=pltpu.CompilerParams(
                collective_id=0, has_side_effects=True, vmem_limit_bytes=60 * 2**20
            ),
            name="adjoint_step",
        )(record_choice_table, sensitivity_heat, stored_heat, friction_diagonal, stored_motions)
        layer = pl.BlockSpec((1, rows, width), lambda l: (l, 0, 0))
        return pl.pallas_call(
            finish,
            grid=(layers,),
            out_shape=(
                jax.ShapeDtypeStruct((layers, rows, width), f32),
                jax.ShapeDtypeStruct((3, layers, rows, width), f32),
            ),
            in_specs=[
                pl.BlockSpec((8, 128), lambda l: (0, 0)),
                layer,
                pl.BlockSpec((3, 3, 1, rows, width), lambda l: (0, 0, l, 0, 0)),
            ],
            out_specs=(layer, pl.BlockSpec((3, 1, rows, width), lambda l: (0, l, 0, 0))),
            compiler_params=pltpu.CompilerParams(vmem_limit_bytes=60 * 2**20),
            name="finish",
        )(coefficients, advected, zs)

    placed = (
        P("rad", "sub", "dia"),
        P("rad", "sub", "dia"),
        P("rad", "sub", "dia"),
        P(None, None, "rad", "sub", "dia"),
        P("dia"),
    )
    return jax.shard_map(
        shards,
        mesh=mesh,
        in_specs=placed,
        out_specs=(P("rad", "sub", "dia"), P(None, "rad", "sub", "dia")),
        check_vma=False,
    )
```

```python
import functools

import jax
import jax.numpy as jnp
from jax import lax
from jax.experimental import pallas as pl
from jax.experimental.pallas import tpu as pltpu
from jax.sharding import PartitionSpec as P

MESH = pl.DeviceIdType.MESH
H = 4
Y_COUNT, CORES = 4, 2
ALPHA_LOW, ALPHA_HIGH = 0.5, 62.0


def later(x, axis):
    return pltpu.roll(x, x.shape[axis] - 1, axis)


def earlier(x, axis):
    return pltpu.roll(x, 1, axis)


def places(sizes):
    n_dia, n_sub, n_rad, n_y, n_core = sizes
    n_zh = n_sub // (n_y * n_core)
    dia, sub, rad = lax.axis_index("dia"), lax.axis_index("sub"), lax.axis_index("rad")
    y, zh, core = sub // (n_zh * n_core), (sub // n_core) % n_zh, sub % n_core
    n_z = n_zh * n_dia
    n_g = n_rad * n_y * n_core
    z = zh * n_dia + dia
    g = (rad * n_y + y) * n_core + core

    def along_z(k):
        t = lax.rem(z + k, n_z)
        return {"sub": (y * n_zh + t // n_dia) * n_core + core, "dia": t % n_dia}

    def in_plane(k):
        t = lax.rem(g + k, n_g)
        r2, y2, c2 = t // (n_y * n_core), (t // n_core) % n_y, t % n_core
        return {"sub": (y2 * n_zh + zh) * n_core + c2, "rad": r2}

    return dia, sub, rad, core, z, g, n_z, n_g, along_z, in_plane


def kernel(
    sizes, table, s_hbm, t_hbm, f_hbm, m_hbm, adv_hbm, zs_hbm, coef_ref,
    s_v, d_v, m_v, T, Q, I, z0, z1, z2, eu0, ed0,
    sub_out, sub_in, dia_out, dia_in, fwd_out, fwd_in, mine, plane, column, temp_v,
    load_sem, store_sem, dia_s, dia_r, rad_s, rad_r, sub_s, sub_r, cor_s, cor_r, fwd_s, fwd_r, late_s, late_r, edge_s, edge_r,
    plane_s, plane_r, column_s, column_r, relay,
):
    n_dia, n_sub, n_rad, n_y, n_core = sizes
    layers, rows, width = s_v.shape
    full_rows, full = rows + 8, width + 128
    dia, sub, rad, core, z, g, n_z, n_g, along_z, in_plane = places(sizes)
    reach = max(1, n_z // 4)
    own = pl.ds(H, layers)
    near = sorted((k for k in range(1, n_z) if min(k, n_z - k) <= reach), key=lambda k: -min(k, n_z - k))

    has_up, has_down = sub < n_sub - 1, sub > 0
    has_above, has_below = rad < n_rad - 1, rad > 0
    above, below = {"rad": jnp.minimum(rad + 1, n_rad - 1)}, {"rad": jnp.maximum(rad - 1, 0)}
    up, down = {"sub": jnp.minimum(sub + 1, n_sub - 1)}, {"sub": jnp.maximum(sub - 1, 0)}
    right, left = {"dia": lax.rem(dia + 1, n_dia)}, {"dia": lax.rem(dia + n_dia - 1, n_dia)}

    barrier = pltpu.get_barrier_semaphore()
    far_up = jnp.logical_and(core == n_core - 1, has_up)
    far_down = jnp.logical_and(core == 0, has_down)

    @pl.when(far_up)
    def _():
        pl.semaphore_signal(barrier, inc=1, device_id=up, device_id_type=MESH)

    @pl.when(far_down)
    def _():
        pl.semaphore_signal(barrier, inc=1, device_id=down, device_id_type=MESH)

    for k in near:
        pl.semaphore_signal(barrier, inc=1, device_id=along_z(k), device_id_type=MESH)

    loads = [
        pltpu.make_async_copy(s_hbm, s_v, load_sem.at[0]),
        pltpu.make_async_copy(f_hbm, d_v, load_sem.at[1]),
        pltpu.make_async_copy(t_hbm, T.at[own, pl.ds(0, rows), pl.ds(0, width)], load_sem.at[2]),
        pltpu.make_async_copy(m_hbm, m_v, load_sem.at[3]),
    ]
    for copy in loads:
        copy.start()
    for k in range(1, n_g):
        pl.semaphore_signal(barrier, inc=1, device_id=in_plane(k), device_id_type=MESH)
    for copy in loads:
        copy.wait()

    lane = lax.broadcasted_iota(jnp.int32, (1, width), 1)
    picks = [table[i] for i in range(2)]
    choice = jnp.where(lane < width // 2, picks[0], picks[1])

    def motion(c, layer, row=slice(None)):
        return jnp.where(
            choice == 0,
            m_v[0, c, layer].astype(jnp.float32)[row],
            m_v[1, c, layer].astype(jnp.float32)[row],
        )

    def prepare(layer, carry):
        s = s_v[layer]
        diagonal = 6.0 + d_v[layer]
        d_v[layer] = diagonal
        inverse = 1.0 / diagonal
        I[H + layer, :rows, :width] = inverse
        Q[H + layer, :rows, :width] = -0.5 * s * inverse
        v = motion(0, layer)
        eu0[layer + 1] = (0.25 + 0.125 * v) * s
        ed0[layer + 1] = (0.25 - 0.125 * v) * s
        return carry

    lax.fori_loop(0, layers, prepare, 0)

    def row_plan(way):
        if way == 0:
            t, q, i = (rows - 3, rows + 5, 3), (rows - 2, rows + 6, 2), (rows - 1, rows + 7, 1)
            deep = ((T, rows - 4, rows + 4), (Q, rows - 3, rows + 5), (I, rows - 2, rows + 6))
            deeper = range(layers // 2, layers)
        else:
            t, q, i = (0, rows, 3), (0, rows, 2), (0, rows, 1)
            deep = ((T, 3, rows + 3), (Q, 2, rows + 2), (I, 1, rows + 1))
            deeper = range(layers // 2)
        plan = []
        for pair in range(layers // 2):
            plan += [(T, 2 * pair, *t), (T, 2 * pair + 1, *t), (Q, 2 * pair, *q)]
        for pair in range(layers // 2):
            plan.append((Q, 2 * pair + 1, *q))
        plan += [(I, l, *i) for l in range(layers)]
        for l in deeper:
            plan += [(ref, l, src, dst, 1) for ref, src, dst in deep]
        at, placed = 0, []
        for ref, l, src, dst, count in plan:
            placed.append((ref, H + l, src, dst, count, at // 8, at % 8))
            at += count
        return placed

    def pack(columns):
        for way in range(2):
            for ref, L, src, _, count, tile, at in row_plan(way):
                sub_out[way, tile, at : at + count, columns] = ref[L, src : src + count, columns]

    def pack_edges():
        for l in range(layers):
            v = motion(1, l)
            s = s_v[l]
            sub_out[0, layers, l : l + 1, :width] = ((0.25 - 0.125 * v) * s)[rows - 1 : rows]
            sub_out[1, layers, l : l + 1, :width] = ((0.25 + 0.125 * v) * s)[0:1]

    main, side = slice(0, width), slice(width, full)
    pack(main)
    pack_edges()

    tile_lane = lax.broadcasted_iota(jnp.int32, (1, 128), 1)
    packed = [jnp.zeros((8, 128), jnp.float32), jnp.zeros((8, 128), jnp.float32)]
    for l in range(layers):
        for half in range(rows // 8):
            k = l * (rows // 8) + half
            group = slice(8 * half, 8 * half + 8)
            for side_at, at in ((0, slice(width - 128, width)), (1, slice(0, 128))):
                pick = picks[1] if side_at == 0 else picks[0]
                v = jnp.where(
                    pick == 0,
                    m_v[0, 2, l, :, at].astype(jnp.float32)[group],
                    m_v[1, 2, l, :, at].astype(jnp.float32)[group],
                )
                sign = -0.125 if side_at == 0 else 0.125
                e = (0.25 + sign * v) * s_v[l, group, at]
                items = (T[H + l, group, at], Q[H + l, group, at], I[H + l, group, at], e)
                tile = packed[side_at]
                for n, item in enumerate(items):
                    if side_at == 0:
                        low = 124 - 4 * n - 16 * k
                        moved = pltpu.roll(item, (low - 124) % 128, 1)
                    else:
                        low = 4 * n + 16 * k
                        moved = pltpu.roll(item, low % 128, 1)
                    tile = jnp.where((tile_lane >= low) & (tile_lane < low + 4), moved, tile)
                packed[side_at] = tile
    dia_out[0] = packed[0]
    dia_out[1] = packed[1]

    halo_low, halo_high = pl.ds(0, H), pl.ds(H + layers, H)

    @pl.when(jnp.logical_not(has_below))
    def _():
        fwd_in[0] = jnp.zeros(fwd_in.shape[1:], jnp.float32)
        for ref in (T, Q, I):
            ref[halo_low] = jnp.zeros((H, full_rows, full), jnp.float32)
        ed0[0] = jnp.zeros((rows, width), jnp.float32)

    @pl.when(jnp.logical_not(has_above))
    def _():
        fwd_in[1] = jnp.zeros(fwd_in.shape[1:], jnp.float32)
        for ref in (T, Q, I):
            ref[halo_high] = jnp.zeros((H, full_rows, full), jnp.float32)
        eu0[layers + 1] = jnp.zeros((rows, width), jnp.float32)

    @pl.when(jnp.logical_not(has_down))
    def _():
        sub_in[0] = jnp.zeros(sub_in.shape[1:], jnp.float32)

    @pl.when(jnp.logical_not(has_up))
    def _():
        sub_in[1] = jnp.zeros(sub_in.shape[1:], jnp.float32)

    pl.semaphore_wait(
        barrier, len(near) + n_g - 1 + far_up.astype(jnp.int32) + far_down.astype(jnp.int32)
    )

    def send(src, dst, ssem, rsem, device):
        return pltpu.make_async_remote_copy(
            src_ref=src, dst_ref=dst, send_sem=ssem, recv_sem=rsem,
            device_id=device, device_id_type=MESH,
        )

    sub_main = [
        send(sub_out.at[i, pl.ds(0, layers), :, pl.ds(0, width)], sub_in.at[i, pl.ds(0, layers), :, pl.ds(0, width)], sub_s.at[i], sub_r.at[i], to)
        for i, to in enumerate((up, down))
    ]
    sub_side = [
        send(sub_out.at[i, pl.ds(0, layers - 1), :, pl.ds(width, 128)], sub_in.at[i, pl.ds(0, layers - 1), :, pl.ds(width, 128)], cor_s.at[i], cor_r.at[i], to)
        for i, to in enumerate((up, down))
    ]
    sub_edge = [
        send(sub_out.at[i, layers, :, pl.ds(0, width)], sub_in.at[i, layers, :, pl.ds(0, width)], edge_s.at[i], edge_r.at[i], to)
        for i, to in enumerate((up, down))
    ]
    dia_copies = [
        send(dia_out.at[i], dia_in.at[i], dia_s.at[i], dia_r.at[i], to)
        for i, to in enumerate((right, left))
    ]

    def slab(ref, first, count, rows_at, lanes_at):
        return ref.at[pl.ds(first, count), pl.ds(*rows_at), pl.ds(*lanes_at)]

    def layer_copies(counts, rows_at, lanes_at, ssem, rsem, ahead=0):
        both = [[], []]
        for n, (ref, count) in enumerate(zip((T, Q, I), counts)):
            skip = (3 - n) if ahead else 0
            both[0].append(send(
                slab(ref, H + layers - count - skip, count, rows_at[0], lanes_at),
                slab(ref, H - count - skip, count, rows_at[0], lanes_at),
                ssem.at[0, n], rsem.at[0, n], above,
            ))
            both[1].append(send(
                slab(ref, H + skip, count, rows_at[1], lanes_at),
                slab(ref, H + layers + skip, count, rows_at[1], lanes_at),
                ssem.at[1, n], rsem.at[1, n], below,
            ))
        return both

    all_rows = ((0, rows), (0, rows))
    rad_main = layer_copies((3, 2, 1), all_rows, (0, width), rad_s.at[0], rad_r.at[0])
    rad_deep = layer_copies((1, 1, 1), ((8, 8), (0, 8)), (0, width), rad_s.at[1], rad_r.at[1], 1)
    rad_side = layer_copies((3, 2, 1), all_rows, (width, 128), fwd_s, fwd_r)
    rad_edge = [
        [send(ed0.at[layers], ed0.at[0], edge_s.at[2], edge_r.at[2], above)],
        [send(eu0.at[1], eu0.at[layers + 1], edge_s.at[3], edge_r.at[3], below)],
    ]
    rad_rows = [
        [send(fwd_out.at[i], fwd_in.at[i], late_s.at[i], late_r.at[i], to)]
        for i, to in enumerate((above, below))
    ]

    def corner_plan(way):
        far = (rows, 1) if way == 0 else (rows + 7, -1)
        near_side = (rows + 7, -1) if way == 0 else (rows, 1)

        def run(side, depth):
            return (side[0] if side[1] > 0 else side[0] - depth + 1, depth)

        plan = [(T, 1, *run(far, 3)), (T, 2, *run(far, 2)), (Q, 1, *run(far, 2)), (T, 3, *run(far, 1))]
        plan += [(T, 1, *run(near_side, 2)), (Q, 2, *run(far, 1)), (I, 1, *run(far, 1))]
        plan += [(T, 2, *run(near_side, 1)), (Q, 1, *run(near_side, 1))]
        at, placed = 0, []
        for ref, depth, first_row, count in plan:
            src = H + layers - depth if way == 0 else H + depth - 1
            dst = H - depth if way == 0 else H + layers + depth - 1
            placed.append((ref, src, dst, first_row, count, at // 8, at % 8))
            at += count
        return placed

    def start(copies, flag):
        @pl.when(flag)
        def _():
            for copy in copies:
                copy.start()

    def arrived(copies, flag):
        @pl.when(flag)
        def _():
            for copy in copies:
                copy.wait_recv()

    def left_here(copies, flag):
        @pl.when(flag)
        def _():
            for copy in copies:
                copy.wait_send()

    start([sub_main[0]], has_up)
    start([sub_main[1]], has_down)
    for copy in dia_copies:
        copy.start()
    for group in (rad_main, rad_deep):
        start(group[0], has_above)
        start(group[1], has_below)

    for k in sorted({reach, n_z - reach}):
        pl.semaphore_signal(relay, inc=1, device_id=along_z(k), device_id_type=MESH)

    for copy in dia_copies:
        copy.wait_recv()
    for l in range(layers):
        for half in range(rows // 8):
            k = l * (rows // 8) + half
            group = slice(8 * half, 8 * half + 8)
            for n, ref in enumerate((T, Q, I)):
                from_left = pltpu.roll(dia_in[0], (4 * n + 16 * k) % 128, 1)
                from_right = pltpu.roll(dia_in[1], (-4 * n - 16 * k) % 128, 1)
                ref[H + l, group, width:full] = jnp.where(tile_lane < 64, from_right, from_left)
    pack(side)
    start([sub_side[0]], has_up)
    start([sub_side[1]], has_down)
    start(rad_side[0], has_above)
    start(rad_side[1], has_below)
    start([sub_edge[0]], has_up)
    start([sub_edge[1]], has_down)
    start(rad_edge[0], has_above)
    start(rad_edge[1], has_below)

    def unpack(columns):
        for way in range(2):
            for ref, L, _, dst, count, tile, at in row_plan(way):
                ref[L, dst : dst + count, columns] = sub_in[way, tile, at : at + count, columns]

    low_half, high_half, every = slice(0, 8), slice(8, 16), slice(0, full_rows)
    inner, outer = slice(0, rows), slice(rows, full_rows)
    bottom, top = H - 1, H + layers

    def across_layers(L, at):
        z0[0, L, at] = Q[L, at] * (T[L + 1, at] - T[L - 1, at])

    def across_rows(L, at):
        t = T[L]
        z0[1, L, at] = Q[L, at] * (later(t, 0) - earlier(t, 0))[at]

    def across_columns(L, at):
        t = T[L, at]
        z0[2, L, at] = Q[L, at] * (later(t, 1) - earlier(t, 1))

    def column_sum(ref, c, L, at):
        x = ref[c, L, at]
        return later(x, 1) + earlier(x, 1)

    def other_sum(ref, c, L, at):
        x = ref[c, L]
        return ref[c, L + 1, at] + ref[c, L - 1, at] + (later(x, 0) + earlier(x, 0))[at]

    def over_layers(step, beyond, at, deep=True):
        lax.fori_loop(bottom - beyond + 1, top + beyond, lambda L, carry: (step(L, at), carry)[1], 0)
        if deep:
            step(bottom - beyond, high_half)
            step(top + beyond, low_half)

    for group in (rad_main, rad_deep, rad_side):
        arrived(group[0], has_below)
        arrived(group[1], has_above)

    def early(L, at):
        across_layers(L, at)
        across_columns(L, at)

    def early_sums(L, at):
        for c in (0, 2):
            z1[c, L, at] = column_sum(z0, c, L, at)

    over_layers(early, 2, inner)
    over_layers(early_sums, 1, inner)

    arrived([sub_main[0]], has_down)
    arrived([sub_main[1]], has_up)
    unpack(main)
    arrived([sub_side[0]], has_down)
    arrived([sub_side[1]], has_up)
    unpack(side)
    for way in range(2):
        for ref, src, _, row_at, count, tile, at in corner_plan(way):
            fwd_out[way, tile, at : at + count] = ref[src, row_at : row_at + count]
    start(rad_rows[0], has_above)
    start(rad_rows[1], has_below)

    def late(L, carry):
        across_layers(L, outer)
        across_columns(L, outer)
        across_rows(L, every)
        return carry

    lax.fori_loop(H + 1, H + layers - 1, late, 0)
    arrived(rad_rows[0], has_below)
    arrived(rad_rows[1], has_above)
    for way in range(2):
        for ref, _, dst, row_at, count, tile, at in corner_plan(way):
            ref[dst, row_at : row_at + count] = fwd_in[way, tile, at : at + count]

    lax.fori_loop(bottom - 1, H + 1, late, 0)
    lax.fori_loop(H + layers - 1, top + 2, late, 0)
    across_rows(bottom - 2, high_half)
    across_rows(top + 2, low_half)

    def second(L, at):
        for c in (0, 2):
            z1[c, L, at] = I[L, at] * (z1[c, L, at] + other_sum(z0, c, L, at))
        z1[1, L, at] = I[L, at] * (column_sum(z0, 1, L, at) + other_sum(z0, 1, L, at))

    def second_outer(L, at):
        for c in (0, 2):
            z1[c, L, at] = I[L, at] * (column_sum(z0, c, L, at) + other_sum(z0, c, L, at))
        z1[1, L, at] = I[L, at] * (column_sum(z0, 1, L, at) + other_sum(z0, 1, L, at))

    def third(L, at):
        for c in range(3):
            z2[c, L, at] = I[L, at] * (column_sum(z1, c, L, at) + other_sum(z1, c, L, at))

    over_layers(second, 1, inner)
    over_layers(second_outer, 1, outer, False)
    over_layers(third, 0, every)

    def folded(x):
        total = jnp.zeros((8, 128), jnp.float32)
        for r in range(0, rows, 8):
            for w in range(0, width, 128):
                total = total + x[r : r + 8, w : w + 128]
        return total

    row_at = lax.broadcasted_iota(jnp.int32, (rows, width), 0)

    def moments(l, sums):
        L = H + l
        d = d_v[l]
        new = [0.0] * 6
        for c in range(3):
            a, b, e = z0[c, L, :rows, :width], z1[c, L, :rows, :width], z2[c, L, :rows, :width]
            x = z2[c, L]
            ahead = jnp.where((row_at < 8) | (l < layers - 1), z2[c, L + 1, :rows, :width], 0.0)
            ahead += jnp.where((row_at < rows - 1) | (l < layers // 2), later(x, 0)[:rows, :width], 0.0)
            ahead += jnp.where((row_at == 0) & (l >= layers // 2), earlier(x, 0)[:rows, :width], 0.0)
            ahead += later(x[:rows], 1)[:, :width]
            da, db, de = d * a, d * b, d * e
            for j, term in enumerate((da * a, da * b, db * b, db * e, de * e, e * ahead)):
                new[j] = new[j] + term
        return tuple(total + folded(x) for total, x in zip(sums, new))

    sums = list(lax.fori_loop(0, layers, moments, (jnp.zeros((8, 128), jnp.float32),) * 6))
    for c in range(3):
        joint = z2[c, H, high_half, :width] * z2[c, bottom, high_half, :width]
        for w in range(0, width, 128):
            sums[5] = sums[5] + joint[:, w : w + 128]
    sums[5] = 2.0 * sums[5]

    row = jnp.zeros((1, 128), jnp.float32)
    for j in range(6):
        row = jnp.where(tile_lane == j, jnp.sum(sums[j], keepdims=True), row)

    def exchange(value, slots, count, index, peer, ssem, rsem, order):
        mine[...] = value
        slots[index] = value
        for k in order:
            send(mine, slots.at[index], ssem, rsem, peer(k)).start()
        return send(slots.at[pl.ds(0, count - 1)], slots.at[pl.ds(0, count - 1)], ssem, rsem, peer(1))

    copies = exchange(row, plane, n_g, g, in_plane, plane_s, plane_r, range(1, n_g))
    stores = [
        pltpu.make_async_copy(ref.at[:, own, pl.ds(0, rows), pl.ds(0, width)], zs_hbm.at[k], store_sem.at[k])
        for k, ref in enumerate((z0, z1, z2))
    ]
    copies.wait_recv()
    copies.wait_send()
    row = jnp.sum(plane[...], axis=0)
    far_first = sorted(range(1, n_z), key=lambda k: -min(k, n_z - k))
    pl.semaphore_wait(relay, len({reach, n_z - reach}))
    copies = exchange(row, column, n_z, z, along_z, column_s, column_r, far_first)

    for copy in stores:
        copy.start()
    arrived([sub_edge[0]], has_down)
    arrived([sub_edge[1]], has_up)
    arrived(rad_edge[0], has_below)
    arrived(rad_edge[1], has_above)

    def advect(l, carry):
        s = s_v[l]
        v1, v2 = motion(1, l), motion(2, l)
        total = -0.5 * s + eu0[l + 2] + ed0[l]
        u, w = (0.25 + 0.125 * v1) * s, (0.25 - 0.125 * v1) * s
        total = total + jnp.where(row_at == rows - 1, sub_in[1, layers, pl.ds(l, 1), :width], later(u, 0))
        total = total + jnp.where(row_at == 0, sub_in[0, layers, pl.ds(l, 1), :width], earlier(w, 0))
        u, w = (0.25 + 0.125 * v2) * s, (0.25 - 0.125 * v2) * s
        temp_v[l] = total + later(u, 1) + earlier(w, 1)
        return carry

    lax.fori_loop(0, layers, advect, 0)
    for l in range(layers):
        for half in range(rows // 8):
            k = l * (rows // 8) + half
            group = slice(8 * half, 8 * half + 8)
            s_low, s_high = s_v[l, group, 0:128], s_v[l, group, width - 128 : width]

            def speed(at, pick, group=group, l=l):
                return jnp.where(
                    pick == 0,
                    m_v[0, 2, l, :, at].astype(jnp.float32)[group],
                    m_v[1, 2, l, :, at].astype(jnp.float32)[group],
                )

            low, high = slice(0, 128), slice(width - 128, width)
            u = pltpu.roll((0.25 + 0.125 * speed(low, picks[0])) * s_low, 127, 1)
            w = pltpu.roll((0.25 - 0.125 * speed(high, picks[1])) * s_high, 1, 1)
            from_left = pltpu.roll(dia_in[0], (13 + 16 * k) % 128, 1)
            from_right = pltpu.roll(dia_in[1], (127 - 12 - 16 * k) % 128, 1)
            temp_v[l, group, low] += jnp.where(tile_lane == 0, from_left - w, 0.0)
            temp_v[l, group, high] += jnp.where(tile_lane == 127, from_right - u, 0.0)

    stores.append(pltpu.make_async_copy(temp_v, adv_hbm, store_sem.at[3]))
    stores[3].start()
    left_here([sub_main[0], sub_side[0], sub_edge[0]], has_up)
    left_here([sub_main[1], sub_side[1], sub_edge[1]], has_down)
    for copy in dia_copies:
        copy.wait_send()
    for group in (rad_main, rad_deep, rad_side, rad_rows, rad_edge):
        left_here(group[0], has_above)
        left_here(group[1], has_below)
    for copy in stores:
        copy.wait()

    copies.wait_recv()
    copies.wait_send()
    row = jnp.sum(column[...], axis=0)
    m0, m1, m2, m3, m4, m5 = (
        jnp.sum(jnp.where(tile_lane == j, row, 0.0), axis=1, keepdims=True) for j in range(6)
    )

    def step(p):
        a, b, c = p
        square = (a * a, 2.0 * a * b, b * b + 2.0 * a * c, 2.0 * b * c, c * c)
        energy = sum(x * m for x, m in zip(square, (m0, m1, m2, m3, m4)))
        moved = sum(x * m for x, m in zip(square, (m1, m2, m3, m4, m5)))
        return jnp.clip(energy / (energy - moved), ALPHA_LOW, ALPHA_HIGH)

    one, none = jnp.ones_like(m0), jnp.zeros_like(m0)
    p0 = (one, none, none)
    alpha0 = step(p0)
    p1 = (1.0 - alpha0, alpha0, none)
    alpha1 = step(p1)
    p2 = (p1[0] * (1.0 - alpha1), p1[1] * (1.0 - alpha1) + p1[0] * alpha1, p1[1] * alpha1)
    alpha2 = step(p2)
    c0, c1, c2 = (alpha0 * x + alpha1 * y + alpha2 * w for x, y, w in zip(p0, p1, p2))

    wide = jnp.zeros((8, 128), jnp.float32)
    row_of = lax.broadcasted_iota(jnp.int32, (8, 128), 0)
    for n, value in enumerate((c0, c1, c2)):
        wide = jnp.where(row_of == n, value, wide)
    coef_ref[...] = wide


def finish(coef_hbm, adv_hbm, zs_hbm, temp_hbm, vel_hbm, coef, adv, zs, temp, vel, load_sem, store_sem):
    layers = adv.shape[0]
    loads, stores = [pltpu.make_async_copy(coef_hbm, coef, load_sem.at[2, 0])], []
    loads[0].start()
    for l in range(layers):
        loads.append(pltpu.make_async_copy(zs_hbm.at[:, :, l], zs.at[:, :, l], load_sem.at[0, l]))
        loads.append(pltpu.make_async_copy(adv_hbm.at[l], adv.at[l], load_sem.at[1, l]))
        stores.append(pltpu.make_async_copy(vel.at[:, l], vel_hbm.at[:, l], store_sem.at[0, l]))
        stores.append(pltpu.make_async_copy(temp.at[l], temp_hbm.at[l], store_sem.at[1, l]))
        loads[-2].start()
        loads[-1].start()
    loads[0].wait()
    c0, c1, c2 = (coef[n : n + 1, 0:1] for n in range(3))
    for l in range(layers):
        loads[2 * l + 1].wait()
        loads[2 * l + 2].wait()
        for c in range(3):
            velocity = c0 * zs[0, c, l] + c1 * zs[1, c, l] + c2 * zs[2, c, l]
            vel[c, l] = velocity
            if c == 0:
                temp[l] = adv[l] + 4.0 * velocity
        stores[2 * l].start()
        stores[2 * l + 1].start()
    for copy in stores:
        copy.wait()


def solution(mesh):
    shape = mesh.shape
    n_y = Y_COUNT if shape["sub"] >= 32 else 1
    sizes = (shape["dia"], shape["sub"], shape["rad"], n_y, CORES)
    n_z = shape["dia"] * shape["sub"] // (n_y * CORES)
    n_g = shape["rad"] * n_y * CORES

    def shards(sensitivity_heat, stored_heat, friction_diagonal, stored_motions, record_choice_table):
        layers, rows, width = sensitivity_heat.shape
        tall, wide, long = layers + 2 * H, rows + 8, width + 128
        f32 = jnp.float32
        block = pltpu.VMEM((layers, rows, width), f32)
        field = pltpu.VMEM((tall, wide, long), f32)
        vector = pltpu.VMEM((3, tall, wide, long), f32)
        dma = pltpu.SemaphoreType.DMA
        in_hbm = pl.BlockSpec(memory_space=pltpu.HBM)
        advected, zs, coefficients = pl.pallas_call(
            functools.partial(kernel, sizes),
            out_shape=(
                jax.ShapeDtypeStruct((layers, rows, width), f32),
                jax.ShapeDtypeStruct((3, 3, layers, rows, width), f32),
                jax.ShapeDtypeStruct((8, 128), f32),
            ),
            in_specs=[pl.BlockSpec(memory_space=pltpu.SMEM)] + [in_hbm] * 4,
            out_specs=(in_hbm, in_hbm, pl.BlockSpec(memory_space=pltpu.VMEM)),
            scratch_shapes=[
                block, block, pltpu.VMEM(stored_motions.shape, stored_motions.dtype),
                field, field, field, vector, vector, vector,
                pltpu.VMEM((layers + 2, rows, width), f32), pltpu.VMEM((layers + 2, rows, width), f32),
                pltpu.VMEM((2, layers + 1, 8, long), f32), pltpu.VMEM((2, layers + 1, 8, long), f32),
                pltpu.VMEM((2, 8, 128), f32), pltpu.VMEM((2, 8, 128), f32),
                pltpu.VMEM((2, 2, 8, long), f32), pltpu.VMEM((2, 2, 8, long), f32),
                pltpu.VMEM((1, 128), f32), pltpu.VMEM((n_g, 1, 128), f32), pltpu.VMEM((n_z, 1, 128), f32),
                block,
                dma((4,)), dma((4,)), dma((2,)), dma((2,)), dma((2, 2, 3)), dma((2, 2, 3)),
                dma((2,)), dma((2,)), dma((2,)), dma((2,)), dma((2, 3)), dma((2, 3)),
                dma((2,)), dma((2,)), dma((4,)), dma((4,)),
                dma, dma, dma, dma, pltpu.SemaphoreType.REGULAR,
            ],
            compiler_params=pltpu.CompilerParams(
                collective_id=0, has_side_effects=True, vmem_limit_bytes=60 * 2**20
            ),
            name="adjoint_step",
        )(record_choice_table, sensitivity_heat, stored_heat, friction_diagonal, stored_motions)
        return pl.pallas_call(
            finish,
            out_shape=(
                jax.ShapeDtypeStruct((layers, rows, width), f32),
                jax.ShapeDtypeStruct((3, layers, rows, width), f32),
            ),
            in_specs=[in_hbm] * 3,
            out_specs=(in_hbm, in_hbm),
            scratch_shapes=[
                pltpu.VMEM((8, 128), f32), block, pltpu.VMEM((3, 3, layers, rows, width), f32),
                block, pltpu.VMEM((3, layers, rows, width), f32), dma((3, layers)), dma((2, layers)),
            ],
            compiler_params=pltpu.CompilerParams(vmem_limit_bytes=60 * 2**20),
            name="finish",
        )(coefficients, advected, zs)

    placed = (
        P("rad", "sub", "dia"),
        P("rad", "sub", "dia"),
        P("rad", "sub", "dia"),
        P(None, None, "rad", "sub", "dia"),
        P("dia"),
    )
    return jax.shard_map(
        shards,
        mesh=mesh,
        in_specs=placed,
        out_specs=(P("rad", "sub", "dia"), P(None, "rad", "sub", "dia")),
        check_vma=False,
    )
```

```python
import functools

import jax
import jax.numpy as jnp
from jax import lax
from jax.experimental import pallas as pl
from jax.experimental.pallas import tpu as pltpu
from jax.sharding import PartitionSpec as P

MESH = pl.DeviceIdType.MESH
H = 4
Y_COUNT, CORES = 4, 2
ALPHA_LOW, ALPHA_HIGH = 0.5, 62.0


def later(x, axis):
    return pltpu.roll(x, x.shape[axis] - 1, axis)


def earlier(x, axis):
    return pltpu.roll(x, 1, axis)


def places(sizes):
    n_dia, n_sub, n_rad, n_y, n_core = sizes
    n_zh = n_sub // (n_y * n_core)
    dia, sub, rad = lax.axis_index("dia"), lax.axis_index("sub"), lax.axis_index("rad")
    y, zh, core = sub // (n_zh * n_core), (sub // n_core) % n_zh, sub % n_core
    n_z = n_zh * n_dia
    n_g = n_rad * n_y * n_core
    z = zh * n_dia + dia
    g = (rad * n_y + y) * n_core + core

    def along_z(k):
        t = lax.rem(z + k, n_z)
        return {"sub": (y * n_zh + t // n_dia) * n_core + core, "dia": t % n_dia}

    def in_plane(k):
        t = lax.rem(g + k, n_g)
        r2, y2, c2 = t // (n_y * n_core), (t // n_core) % n_y, t % n_core
        return {"sub": (y2 * n_zh + zh) * n_core + c2, "rad": r2}

    return dia, sub, rad, core, z, g, n_z, n_g, along_z, in_plane


def kernel(
    sizes, table, s_hbm, t_hbm, f_hbm, m_hbm, adv_hbm, zs_hbm, coef_ref,
    s_v, d_v, m_v, T, Q, I, z0, z1, z2, eu0, ed0,
    sub_out, sub_in, dia_out, dia_in, fwd_out, fwd_in, side_out, side_in, mine, plane, column, temp_v,
    load_sem, store_sem, dia_s, dia_r, rad_s, rad_r, sub_s, sub_r, cor_s, cor_r, fwd_s, fwd_r, late_s, late_r, edge_s, edge_r,
    plane_s, plane_r, column_s, column_r, relay,
):
    n_dia, n_sub, n_rad, n_y, n_core = sizes
    layers, rows, width = s_v.shape
    full_rows, full = rows + 8, width + 128
    dia, sub, rad, core, z, g, n_z, n_g, along_z, in_plane = places(sizes)
    reach = max(1, n_z // 4)
    own = pl.ds(H, layers)
    near = sorted((k for k in range(1, n_z) if min(k, n_z - k) <= reach), key=lambda k: -min(k, n_z - k))

    has_up, has_down = sub < n_sub - 1, sub > 0
    has_above, has_below = rad < n_rad - 1, rad > 0
    above, below = {"rad": jnp.minimum(rad + 1, n_rad - 1)}, {"rad": jnp.maximum(rad - 1, 0)}
    up, down = {"sub": jnp.minimum(sub + 1, n_sub - 1)}, {"sub": jnp.maximum(sub - 1, 0)}
    right, left = {"dia": lax.rem(dia + 1, n_dia)}, {"dia": lax.rem(dia + n_dia - 1, n_dia)}

    barrier = pltpu.get_barrier_semaphore()
    far_up = jnp.logical_and(core == n_core - 1, has_up)
    far_down = jnp.logical_and(core == 0, has_down)

    @pl.when(far_up)
    def _():
        pl.semaphore_signal(barrier, inc=1, device_id=up, device_id_type=MESH)

    @pl.when(far_down)
    def _():
        pl.semaphore_signal(barrier, inc=1, device_id=down, device_id_type=MESH)

    for k in near:
        pl.semaphore_signal(barrier, inc=1, device_id=along_z(k), device_id_type=MESH)

    loads = [
        pltpu.make_async_copy(s_hbm, s_v, load_sem.at[0]),
        pltpu.make_async_copy(f_hbm, d_v, load_sem.at[1]),
        pltpu.make_async_copy(t_hbm, T.at[own, pl.ds(0, rows), pl.ds(0, width)], load_sem.at[2]),
        pltpu.make_async_copy(m_hbm, m_v, load_sem.at[3]),
    ]
    for copy in loads:
        copy.start()
    for k in range(1, n_g):
        pl.semaphore_signal(barrier, inc=1, device_id=in_plane(k), device_id_type=MESH)
    for copy in loads:
        copy.wait()

    lane = lax.broadcasted_iota(jnp.int32, (1, width), 1)
    picks = [table[i] for i in range(2)]
    choice = jnp.where(lane < width // 2, picks[0], picks[1])

    def motion(c, layer, row=slice(None)):
        return jnp.where(
            choice == 0,
            m_v[0, c, layer].astype(jnp.float32)[row],
            m_v[1, c, layer].astype(jnp.float32)[row],
        )

    def prepare(layer, carry):
        s = s_v[layer]
        diagonal = 6.0 + d_v[layer]
        d_v[layer] = diagonal
        inverse = 1.0 / diagonal
        I[H + layer, :rows, :width] = inverse
        Q[H + layer, :rows, :width] = -0.5 * s * inverse
        v = motion(0, layer)
        eu0[layer + 1] = (0.25 + 0.125 * v) * s
        ed0[layer + 1] = (0.25 - 0.125 * v) * s
        return carry

    lax.fori_loop(0, layers, prepare, 0)

    def row_plan(way):
        if way == 0:
            t, q, i = (rows - 3, rows + 5, 3), (rows - 2, rows + 6, 2), (rows - 1, rows + 7, 1)
            deep = ((T, rows - 4, rows + 4), (Q, rows - 3, rows + 5), (I, rows - 2, rows + 6))
            deeper = range(layers // 2, layers)
        else:
            t, q, i = (0, rows, 3), (0, rows, 2), (0, rows, 1)
            deep = ((T, 3, rows + 3), (Q, 2, rows + 2), (I, 1, rows + 1))
            deeper = range(layers // 2)
        plan = []
        for pair in range(layers // 2):
            plan += [(T, 2 * pair, *t), (T, 2 * pair + 1, *t), (Q, 2 * pair, *q)]
        for pair in range(layers // 2):
            plan.append((Q, 2 * pair + 1, *q))
        plan += [(I, l, *i) for l in range(layers)]
        for l in deeper:
            plan += [(ref, l, src, dst, 1) for ref, src, dst in deep]
        at, placed = 0, []
        for ref, l, src, dst, count in plan:
            placed.append((ref, H + l, src, dst, count, at // 8, at % 8))
            at += count
        return placed

    def pack(columns):
        for way in range(2):
            for ref, L, src, _, count, tile, at in row_plan(way):
                sub_out[way, tile, at : at + count, columns] = ref[L, src : src + count, columns]

    def pack_edges():
        for l in range(layers):
            v = motion(1, l)
            s = s_v[l]
            sub_out[0, layers, l : l + 1, :width] = ((0.25 - 0.125 * v) * s)[rows - 1 : rows]
            sub_out[1, layers, l : l + 1, :width] = ((0.25 + 0.125 * v) * s)[0:1]

    main, side = slice(0, width), slice(width, full)
    pack(main)
    pack_edges()

    tile_lane = lax.broadcasted_iota(jnp.int32, (1, 128), 1)
    packed = [jnp.zeros((8, 128), jnp.float32), jnp.zeros((8, 128), jnp.float32)]
    for l in range(layers):
        for half in range(rows // 8):
            k = l * (rows // 8) + half
            group = slice(8 * half, 8 * half + 8)
            for side_at, at in ((0, slice(width - 128, width)), (1, slice(0, 128))):
                pick = picks[1] if side_at == 0 else picks[0]
                v = jnp.where(
                    pick == 0,
                    m_v[0, 2, l, :, at].astype(jnp.float32)[group],
                    m_v[1, 2, l, :, at].astype(jnp.float32)[group],
                )
                sign = -0.125 if side_at == 0 else 0.125
                e = (0.25 + sign * v) * s_v[l, group, at]
                items = (T[H + l, group, at], Q[H + l, group, at], I[H + l, group, at], e)
                tile = packed[side_at]
                for n, item in enumerate(items):
                    if side_at == 0:
                        low = 124 - 4 * n - 16 * k
                        moved = pltpu.roll(item, (low - 124) % 128, 1)
                    else:
                        low = 4 * n + 16 * k
                        moved = pltpu.roll(item, low % 128, 1)
                    tile = jnp.where((tile_lane >= low) & (tile_lane < low + 4), moved, tile)
                packed[side_at] = tile
    dia_out[0] = packed[0]
    dia_out[1] = packed[1]

    halo_low, halo_high = pl.ds(0, H), pl.ds(H + layers, H)

    @pl.when(jnp.logical_not(has_below))
    def _():
        fwd_in[0] = jnp.zeros(fwd_in.shape[1:], jnp.float32)
        for ref in (T, Q, I):
            ref[halo_low] = jnp.zeros((H, full_rows, full), jnp.float32)
        ed0[0] = jnp.zeros((rows, width), jnp.float32)

    @pl.when(jnp.logical_not(has_above))
    def _():
        fwd_in[1] = jnp.zeros(fwd_in.shape[1:], jnp.float32)
        for ref in (T, Q, I):
            ref[halo_high] = jnp.zeros((H, full_rows, full), jnp.float32)
        eu0[layers + 1] = jnp.zeros((rows, width), jnp.float32)

    @pl.when(jnp.logical_not(has_down))
    def _():
        sub_in[0] = jnp.zeros(sub_in.shape[1:], jnp.float32)
        side_in[0] = jnp.zeros(side_in.shape[1:], jnp.float32)

    @pl.when(jnp.logical_not(has_up))
    def _():
        sub_in[1] = jnp.zeros(sub_in.shape[1:], jnp.float32)
        side_in[1] = jnp.zeros(side_in.shape[1:], jnp.float32)

    pl.semaphore_wait(
        barrier, len(near) + n_g - 1 + far_up.astype(jnp.int32) + far_down.astype(jnp.int32)
    )

    def send(src, dst, ssem, rsem, device):
        return pltpu.make_async_remote_copy(
            src_ref=src, dst_ref=dst, send_sem=ssem, recv_sem=rsem,
            device_id=device, device_id_type=MESH,
        )

    chunks = (pl.ds(0, width // 2), pl.ds(width // 2, width // 2))
    sub_main = [
        [
            send(sub_out.at[i, pl.ds(0, layers), :, at], sub_in.at[i, pl.ds(0, layers), :, at], sub_s.at[i, j], sub_r.at[i, j], to)
            for j, at in enumerate(chunks)
        ]
        for i, to in enumerate((up, down))
    ]
    sub_side = [
        send(side_out.at[i], side_in.at[i], cor_s.at[i], cor_r.at[i], to)
        for i, to in enumerate((up, down))
    ]
    sub_edge = [
        send(sub_out.at[i, layers, :, pl.ds(0, width)], sub_in.at[i, layers, :, pl.ds(0, width)], edge_s.at[i], edge_r.at[i], to)
        for i, to in enumerate((up, down))
    ]
    dia_copies = [
        send(dia_out.at[i], dia_in.at[i], dia_s.at[i], dia_r.at[i], to)
        for i, to in enumerate((right, left))
    ]

    def slab(ref, first, count, rows_at, lanes_at):
        return ref.at[pl.ds(first, count), pl.ds(*rows_at), pl.ds(*lanes_at)]

    def layer_copies(counts, rows_at, lanes_at, ssem, rsem, ahead=0):
        both = [[], []]
        for n, (ref, count) in enumerate(zip((T, Q, I), counts)):
            skip = (3 - n) if ahead else 0
            both[0].append(send(
                slab(ref, H + layers - count - skip, count, rows_at[0], lanes_at),
                slab(ref, H - count - skip, count, rows_at[0], lanes_at),
                ssem.at[0, n], rsem.at[0, n], above,
            ))
            both[1].append(send(
                slab(ref, H + skip, count, rows_at[1], lanes_at),
                slab(ref, H + layers + skip, count, rows_at[1], lanes_at),
                ssem.at[1, n], rsem.at[1, n], below,
            ))
        return both

    all_rows = ((0, rows), (0, rows))
    rad_main = layer_copies((3, 2, 1), all_rows, (0, width), rad_s.at[0], rad_r.at[0])
    rad_deep = layer_copies((1, 1, 1), ((8, 8), (0, 8)), (0, width), rad_s.at[1], rad_r.at[1], 1)
    rad_side = layer_copies((3, 2, 1), all_rows, (width, 128), fwd_s, fwd_r)
    rad_edge = [
        [send(ed0.at[layers], ed0.at[0], edge_s.at[2], edge_r.at[2], above)],
        [send(eu0.at[1], eu0.at[layers + 1], edge_s.at[3], edge_r.at[3], below)],
    ]
    parts = (pl.ds(0, width // 2), pl.ds(width // 2, full - width // 2))
    rad_rows = [
        [
            send(fwd_out.at[i, :, :, at], fwd_in.at[i, :, :, at], late_s.at[i, j], late_r.at[i, j], to)
            for j, at in enumerate(parts)
        ]
        for i, to in enumerate((above, below))
    ]

    def corner_plan(way):
        far = (rows, 1) if way == 0 else (rows + 7, -1)
        near_side = (rows + 7, -1) if way == 0 else (rows, 1)

        def run(side, depth):
            return (side[0] if side[1] > 0 else side[0] - depth + 1, depth)

        plan = [(T, 1, *run(far, 3)), (T, 2, *run(far, 2)), (Q, 1, *run(far, 2)), (T, 3, *run(far, 1))]
        plan += [(T, 1, *run(near_side, 2)), (Q, 2, *run(far, 1)), (I, 1, *run(far, 1))]
        plan += [(T, 2, *run(near_side, 1)), (Q, 1, *run(near_side, 1))]
        at, placed = 0, []
        for ref, depth, first_row, count in plan:
            src = H + layers - depth if way == 0 else H + depth - 1
            dst = H - depth if way == 0 else H + layers + depth - 1
            placed.append((ref, src, dst, first_row, count, at // 8, at % 8))
            at += count
        return placed

    def start(copies, flag):
        @pl.when(flag)
        def _():
            for copy in copies:
                copy.start()

    def arrived(copies, flag):
        @pl.when(flag)
        def _():
            for copy in copies:
                copy.wait_recv()

    def left_here(copies, flag):
        @pl.when(flag)
        def _():
            for copy in copies:
                copy.wait_send()

    for j in range(2):
        start([sub_main[0][j]], has_up)
        start([sub_main[1][j]], has_down)
    for copy in dia_copies:
        copy.start()
    for group in (rad_main, rad_deep):
        start(group[0], has_above)
        start(group[1], has_below)

    for k in sorted({reach, n_z - reach}):
        pl.semaphore_signal(relay, inc=1, device_id=along_z(k), device_id_type=MESH)

    for copy in dia_copies:
        copy.wait_recv()
    for l in range(layers):
        for half in range(rows // 8):
            k = l * (rows // 8) + half
            group = slice(8 * half, 8 * half + 8)
            for n, ref in enumerate((T, Q, I)):
                from_left = pltpu.roll(dia_in[0], (4 * n + 16 * k) % 128, 1)
                from_right = pltpu.roll(dia_in[1], (-4 * n - 16 * k) % 128, 1)
                ref[H + l, group, width:full] = jnp.where(tile_lane < 64, from_right, from_left)
    pack(side)
    for way in range(2):
        tile = sub_out[way, 0, :, side]
        for k in range(1, layers - 1):
            low = 8 * k - 4
            tile = jnp.where((tile_lane >= low) & (tile_lane < low + 8), pltpu.roll(sub_out[way, k, :, side], 8 * k, 1), tile)
        side_out[way] = tile
    start([sub_side[0]], has_up)
    start([sub_side[1]], has_down)
    start(rad_side[0], has_above)
    start(rad_side[1], has_below)
    start([sub_edge[0]], has_up)
    start([sub_edge[1]], has_down)
    start(rad_edge[0], has_above)
    start(rad_edge[1], has_below)

    def unpack(columns):
        for way in range(2):
            for ref, L, _, dst, count, tile, at in row_plan(way):
                ref[L, dst : dst + count, columns] = sub_in[way, tile, at : at + count, columns]

    low_half, high_half, every = slice(0, 8), slice(8, 16), slice(0, full_rows)
    inner, outer = slice(0, rows), slice(rows, full_rows)
    bottom, top = H - 1, H + layers

    def across_layers(L, at):
        z0[0, L, at] = Q[L, at] * (T[L + 1, at] - T[L - 1, at])

    def across_rows(L, at):
        t = T[L]
        z0[1, L, at] = Q[L, at] * (later(t, 0) - earlier(t, 0))[at]

    def across_columns(L, at):
        t = T[L, at]
        z0[2, L, at] = Q[L, at] * (later(t, 1) - earlier(t, 1))

    def column_sum(ref, c, L, at):
        x = ref[c, L, at]
        return later(x, 1) + earlier(x, 1)

    def other_sum(ref, c, L, at):
        x = ref[c, L]
        return ref[c, L + 1, at] + ref[c, L - 1, at] + (later(x, 0) + earlier(x, 0))[at]

    def over_layers(step, beyond, at, deep=True):
        lax.fori_loop(bottom - beyond + 1, top + beyond, lambda L, carry: (step(L, at), carry)[1], 0)
        if deep:
            step(bottom - beyond, high_half)
            step(top + beyond, low_half)

    def forward(columns, j):
        for way in range(2):
            for ref, src, _, row_at, count, tile, at in corner_plan(way):
                fwd_out[way, tile, at : at + count, columns] = ref[src, row_at : row_at + count, columns]
        start([rad_rows[0][j]], has_above)
        start([rad_rows[1][j]], has_below)

    arrived([sub_main[0][0]], has_down)
    arrived([sub_main[1][0]], has_up)
    unpack(slice(0, width // 2))
    forward(slice(0, width // 2), 0)

    for group in (rad_main, rad_deep, rad_side):
        arrived(group[0], has_below)
        arrived(group[1], has_above)

    def early(L, at):
        across_layers(L, at)
        across_columns(L, at)

    def early_sums(L, at):
        for c in (0, 2):
            z1[c, L, at] = column_sum(z0, c, L, at)

    over_layers(early, 2, inner)
    over_layers(early_sums, 1, inner)

    arrived([sub_main[0][1]], has_down)
    arrived([sub_main[1][1]], has_up)
    unpack(slice(width // 2, width))
    arrived([sub_side[0]], has_down)
    arrived([sub_side[1]], has_up)
    for way in range(2):
        for k in range(layers - 1):
            sub_in[way, k, :, side] = pltpu.roll(side_in[way], (-8 * k) % 128, 1)
    unpack(side)
    forward(slice(width // 2, full), 1)

    def late(L, carry):
        across_layers(L, outer)
        across_columns(L, outer)
        across_rows(L, every)
        return carry

    lax.fori_loop(H + 1, H + layers - 1, late, 0)
    arrived(rad_rows[0], has_below)
    arrived(rad_rows[1], has_above)
    for way in range(2):
        for ref, _, dst, row_at, count, tile, at in corner_plan(way):
            ref[dst, row_at : row_at + count] = fwd_in[way, tile, at : at + count]

    lax.fori_loop(bottom - 1, H + 1, late, 0)
    lax.fori_loop(H + layers - 1, top + 2, late, 0)
    across_rows(bottom - 2, high_half)
    across_rows(top + 2, low_half)

    def second(L, at):
        for c in (0, 2):
            z1[c, L, at] = I[L, at] * (z1[c, L, at] + other_sum(z0, c, L, at))
        z1[1, L, at] = I[L, at] * (column_sum(z0, 1, L, at) + other_sum(z0, 1, L, at))

    def second_outer(L, at):
        for c in (0, 2):
            z1[c, L, at] = I[L, at] * (column_sum(z0, c, L, at) + other_sum(z0, c, L, at))
        z1[1, L, at] = I[L, at] * (column_sum(z0, 1, L, at) + other_sum(z0, 1, L, at))

    def third(L, at):
        for c in range(3):
            z2[c, L, at] = I[L, at] * (column_sum(z1, c, L, at) + other_sum(z1, c, L, at))

    over_layers(second, 1, inner)
    over_layers(second_outer, 1, outer, False)
    over_layers(third, 0, every)

    def folded(x):
        total = jnp.zeros((8, 128), jnp.float32)
        for r in range(0, rows, 8):
            for w in range(0, width, 128):
                total = total + x[r : r + 8, w : w + 128]
        return total

    row_at = lax.broadcasted_iota(jnp.int32, (rows, width), 0)

    def moments(l, sums):
        L = H + l
        d = d_v[l]
        new = [0.0] * 6
        for c in range(3):
            a, b, e = z0[c, L, :rows, :width], z1[c, L, :rows, :width], z2[c, L, :rows, :width]
            x = z2[c, L]
            ahead = jnp.where((row_at < 8) | (l < layers - 1), z2[c, L + 1, :rows, :width], 0.0)
            ahead += jnp.where((row_at < rows - 1) | (l < layers // 2), later(x, 0)[:rows, :width], 0.0)
            ahead += jnp.where((row_at == 0) & (l >= layers // 2), earlier(x, 0)[:rows, :width], 0.0)
            ahead += later(x[:rows], 1)[:, :width]
            da, db, de = d * a, d * b, d * e
            for j, term in enumerate((da * a, da * b, db * b, db * e, de * e, e * ahead)):
                new[j] = new[j] + term
        return tuple(total + folded(x) for total, x in zip(sums, new))

    sums = list(lax.fori_loop(0, layers, moments, (jnp.zeros((8, 128), jnp.float32),) * 6))
    for c in range(3):
        joint = z2[c, H, high_half, :width] * z2[c, bottom, high_half, :width]
        for w in range(0, width, 128):
            sums[5] = sums[5] + joint[:, w : w + 128]
    sums[5] = 2.0 * sums[5]

    row = jnp.zeros((1, 128), jnp.float32)
    for j in range(6):
        row = jnp.where(tile_lane == j, jnp.sum(sums[j], keepdims=True), row)

    def exchange(value, turn, slots, count, index, peer, ssem, rsem, order):
        mine[turn] = value
        slots[index] = value
        for k in order:
            send(mine.at[turn], slots.at[index], ssem, rsem, peer(k)).start()
        return send(slots.at[pl.ds(0, count - 1)], slots.at[pl.ds(0, count - 1)], ssem, rsem, peer(1))

    def hops(k):
        across, along = k // (n_y * n_core), (k // n_core) % n_y
        return min(across, n_rad - across) + min(along, n_y - along)

    far_in_plane = sorted(range(1, n_g), key=lambda k: -hops(k))
    in_plane_copies = exchange(row, 0, plane, n_g, g, in_plane, plane_s, plane_r, far_in_plane)
    stores = [
        pltpu.make_async_copy(ref.at[:, own, pl.ds(0, rows), pl.ds(0, width)], zs_hbm.at[k], store_sem.at[k])
        for k, ref in enumerate((z0, z1, z2))
    ]
    in_plane_copies.wait_recv()
    row = jnp.sum(plane[...], axis=0)
    far_first = sorted(range(1, n_z), key=lambda k: -min(k, n_z - k))
    pl.semaphore_wait(relay, len({reach, n_z - reach}))
    copies = exchange(row, 1, column, n_z, z, along_z, column_s, column_r, far_first)

    for copy in stores:
        copy.start()
    arrived([sub_edge[0]], has_down)
    arrived([sub_edge[1]], has_up)
    arrived(rad_edge[0], has_below)
    arrived(rad_edge[1], has_above)

    def advect(l, carry):
        s = s_v[l]
        v1, v2 = motion(1, l), motion(2, l)
        total = -0.5 * s + eu0[l + 2] + ed0[l]
        u, w = (0.25 + 0.125 * v1) * s, (0.25 - 0.125 * v1) * s
        total = total + jnp.where(row_at == rows - 1, sub_in[1, layers, pl.ds(l, 1), :width], later(u, 0))
        total = total + jnp.where(row_at == 0, sub_in[0, layers, pl.ds(l, 1), :width], earlier(w, 0))
        u, w = (0.25 + 0.125 * v2) * s, (0.25 - 0.125 * v2) * s
        temp_v[l] = total + later(u, 1) + earlier(w, 1)
        return carry

    lax.fori_loop(0, layers, advect, 0)
    for l in range(layers):
        for half in range(rows // 8):
            k = l * (rows // 8) + half
            group = slice(8 * half, 8 * half + 8)
            s_low, s_high = s_v[l, group, 0:128], s_v[l, group, width - 128 : width]

            def speed(at, pick, group=group, l=l):
                return jnp.where(
                    pick == 0,
                    m_v[0, 2, l, :, at].astype(jnp.float32)[group],
                    m_v[1, 2, l, :, at].astype(jnp.float32)[group],
                )

            low, high = slice(0, 128), slice(width - 128, width)
            u = pltpu.roll((0.25 + 0.125 * speed(low, picks[0])) * s_low, 127, 1)
            w = pltpu.roll((0.25 - 0.125 * speed(high, picks[1])) * s_high, 1, 1)
            from_left = pltpu.roll(dia_in[0], (13 + 16 * k) % 128, 1)
            from_right = pltpu.roll(dia_in[1], (127 - 12 - 16 * k) % 128, 1)
            temp_v[l, group, low] += jnp.where(tile_lane == 0, from_left - w, 0.0)
            temp_v[l, group, high] += jnp.where(tile_lane == 127, from_right - u, 0.0)

    stores.append(pltpu.make_async_copy(temp_v, adv_hbm, store_sem.at[3]))
    stores[3].start()
    left_here(sub_main[0] + [sub_side[0], sub_edge[0]], has_up)
    left_here(sub_main[1] + [sub_side[1], sub_edge[1]], has_down)
    for copy in dia_copies:
        copy.wait_send()
    for group in (rad_main, rad_deep, rad_side, rad_rows, rad_edge):
        left_here(group[0], has_above)
        left_here(group[1], has_below)
    for copy in stores:
        copy.wait()
    in_plane_copies.wait_send()

    copies.wait_recv()
    copies.wait_send()
    row = jnp.sum(column[...], axis=0)
    m0, m1, m2, m3, m4, m5 = (
        jnp.sum(jnp.where(tile_lane == j, row, 0.0), axis=1, keepdims=True) for j in range(6)
    )

    def step(p):
        a, b, c = p
        square = (a * a, 2.0 * a * b, b * b + 2.0 * a * c, 2.0 * b * c, c * c)
        energy = sum(x * m for x, m in zip(square, (m0, m1, m2, m3, m4)))
        moved = sum(x * m for x, m in zip(square, (m1, m2, m3, m4, m5)))
        return jnp.clip(energy / (energy - moved), ALPHA_LOW, ALPHA_HIGH)

    one, none = jnp.ones_like(m0), jnp.zeros_like(m0)
    p0 = (one, none, none)
    alpha0 = step(p0)
    p1 = (1.0 - alpha0, alpha0, none)
    alpha1 = step(p1)
    p2 = (p1[0] * (1.0 - alpha1), p1[1] * (1.0 - alpha1) + p1[0] * alpha1, p1[1] * alpha1)
    alpha2 = step(p2)
    c0, c1, c2 = (alpha0 * x + alpha1 * y + alpha2 * w for x, y, w in zip(p0, p1, p2))

    wide = jnp.zeros((8, 128), jnp.float32)
    row_of = lax.broadcasted_iota(jnp.int32, (8, 128), 0)
    for n, value in enumerate((c0, c1, c2)):
        wide = jnp.where(row_of == n, value, wide)
    coef_ref[...] = wide


def finish(coef_hbm, adv_hbm, zs_hbm, temp_hbm, vel_hbm, coef, adv, zs, temp, vel, load_sem, store_sem):
    layers = adv.shape[0]
    loads, stores = [pltpu.make_async_copy(coef_hbm, coef, load_sem.at[2, 0])], []
    loads[0].start()
    for l in range(layers):
        loads.append(pltpu.make_async_copy(zs_hbm.at[:, :, l], zs.at[:, :, l], load_sem.at[0, l]))
        loads.append(pltpu.make_async_copy(adv_hbm.at[l], adv.at[l], load_sem.at[1, l]))
        stores.append(pltpu.make_async_copy(vel.at[:, l], vel_hbm.at[:, l], store_sem.at[0, l]))
        stores.append(pltpu.make_async_copy(temp.at[l], temp_hbm.at[l], store_sem.at[1, l]))
        loads[-2].start()
        loads[-1].start()
    loads[0].wait()
    c0, c1, c2 = (coef[n : n + 1, 0:1] for n in range(3))
    for l in range(layers):
        loads[2 * l + 1].wait()
        loads[2 * l + 2].wait()
        for c in range(3):
            velocity = c0 * zs[0, c, l] + c1 * zs[1, c, l] + c2 * zs[2, c, l]
            vel[c, l] = velocity
            if c == 0:
                temp[l] = adv[l] + 4.0 * velocity
        stores[2 * l].start()
        stores[2 * l + 1].start()
    for copy in stores:
        copy.wait()


def solution(mesh):
    shape = mesh.shape
    n_y = Y_COUNT if shape["sub"] >= 32 else 1
    sizes = (shape["dia"], shape["sub"], shape["rad"], n_y, CORES)
    n_z = shape["dia"] * shape["sub"] // (n_y * CORES)
    n_g = shape["rad"] * n_y * CORES

    def shards(sensitivity_heat, stored_heat, friction_diagonal, stored_motions, record_choice_table):
        layers, rows, width = sensitivity_heat.shape
        tall, wide, long = layers + 2 * H, rows + 8, width + 128
        f32 = jnp.float32
        block = pltpu.VMEM((layers, rows, width), f32)
        field = pltpu.VMEM((tall, wide, long), f32)
        vector = pltpu.VMEM((3, tall, wide, long), f32)
        dma = pltpu.SemaphoreType.DMA
        in_hbm = pl.BlockSpec(memory_space=pltpu.HBM)
        advected, zs, coefficients = pl.pallas_call(
            functools.partial(kernel, sizes),
            out_shape=(
                jax.ShapeDtypeStruct((layers, rows, width), f32),
                jax.ShapeDtypeStruct((3, 3, layers, rows, width), f32),
                jax.ShapeDtypeStruct((8, 128), f32),
            ),
            in_specs=[pl.BlockSpec(memory_space=pltpu.SMEM)] + [in_hbm] * 4,
            out_specs=(in_hbm, in_hbm, pl.BlockSpec(memory_space=pltpu.VMEM)),
            scratch_shapes=[
                block, block, pltpu.VMEM(stored_motions.shape, stored_motions.dtype),
                field, field, field, vector, vector, vector,
                pltpu.VMEM((layers + 2, rows, width), f32), pltpu.VMEM((layers + 2, rows, width), f32),
                pltpu.VMEM((2, layers + 1, 8, long), f32), pltpu.VMEM((2, layers + 1, 8, long), f32),
                pltpu.VMEM((2, 8, 128), f32), pltpu.VMEM((2, 8, 128), f32),
                pltpu.VMEM((2, 2, 8, long), f32), pltpu.VMEM((2, 2, 8, long), f32),
                pltpu.VMEM((2, 8, 128), f32), pltpu.VMEM((2, 8, 128), f32), pltpu.VMEM((2, 1, 128), f32), pltpu.VMEM((n_g, 1, 128), f32), pltpu.VMEM((n_z, 1, 128), f32),
                block,
                dma((4,)), dma((4,)), dma((2,)), dma((2,)), dma((2, 2, 3)), dma((2, 2, 3)),
                dma((2, 2)), dma((2, 2)), dma((2,)), dma((2,)), dma((2, 3)), dma((2, 3)),
                dma((2, 2)), dma((2, 2)), dma((4,)), dma((4,)),
                dma, dma, dma, dma, pltpu.SemaphoreType.REGULAR,
            ],
            compiler_params=pltpu.CompilerParams(
                collective_id=0, has_side_effects=True, vmem_limit_bytes=60 * 2**20
            ),
            name="adjoint_step",
        )(record_choice_table, sensitivity_heat, stored_heat, friction_diagonal, stored_motions)
        return pl.pallas_call(
            finish,
            out_shape=(
                jax.ShapeDtypeStruct((layers, rows, width), f32),
                jax.ShapeDtypeStruct((3, layers, rows, width), f32),
            ),
            in_specs=[in_hbm] * 3,
            out_specs=(in_hbm, in_hbm),
            scratch_shapes=[
                pltpu.VMEM((8, 128), f32), block, pltpu.VMEM((3, 3, layers, rows, width), f32),
                block, pltpu.VMEM((3, layers, rows, width), f32), dma((3, layers)), dma((2, layers)),
            ],
            compiler_params=pltpu.CompilerParams(vmem_limit_bytes=60 * 2**20),
            name="finish",
        )(coefficients, advected, zs)

    placed = (
        P("rad", "sub", "dia"),
        P("rad", "sub", "dia"),
        P("rad", "sub", "dia"),
        P(None, None, "rad", "sub", "dia"),
        P("dia"),
    )
    return jax.shard_map(
        shards,
        mesh=mesh,
        in_specs=placed,
        out_specs=(P("rad", "sub", "dia"), P(None, "rad", "sub", "dia")),
        check_vma=False,
    )
```

```python
import functools

import jax
import jax.numpy as jnp
from jax import lax
from jax.experimental import pallas as pl
from jax.experimental.pallas import tpu as pltpu
from jax.sharding import PartitionSpec as P

MESH = pl.DeviceIdType.MESH
H = 4
Y_COUNT, CORES = 4, 2
ALPHA_LOW, ALPHA_HIGH = 0.5, 62.0


def later(x, axis):
    return pltpu.roll(x, x.shape[axis] - 1, axis)


def earlier(x, axis):
    return pltpu.roll(x, 1, axis)


def places(sizes):
    n_dia, n_sub, n_rad, n_y, n_core = sizes
    n_zh = n_sub // (n_y * n_core)
    dia, sub, rad = lax.axis_index("dia"), lax.axis_index("sub"), lax.axis_index("rad")
    y, zh, core = sub // (n_zh * n_core), (sub // n_core) % n_zh, sub % n_core
    n_z = n_zh * n_dia
    n_g = n_rad * n_y * n_core
    z = zh * n_dia + dia
    g = (rad * n_y + y) * n_core + core

    def along_z(k):
        t = lax.rem(z + k, n_z)
        return {"sub": (y * n_zh + t // n_dia) * n_core + core, "dia": t % n_dia}

    def in_plane(k):
        t = lax.rem(g + k, n_g)
        r2, y2, c2 = t // (n_y * n_core), (t // n_core) % n_y, t % n_core
        return {"sub": (y2 * n_zh + zh) * n_core + c2, "rad": r2}

    return dia, sub, rad, core, z, g, n_z, n_g, along_z, in_plane


def kernel(
    sizes, table, s_hbm, t_hbm, f_hbm, m_hbm, adv_hbm, zs_hbm, coef_ref,
    s_v, d_v, m_v, T, Q, I, z0, z1, z2, trial, eu0, ed0,
    sub_out, sub_in, dia_out, dia_in, fwd_out, fwd_in, side_out, side_in, mine, plane, column, temp_v,
    load_sem, store_sem, dia_s, dia_r, rad_s, rad_r, sub_s, sub_r, cor_s, cor_r, fwd_s, fwd_r, late_s, late_r, edge_s, edge_r,
    plane_s, plane_r, column_s, column_r, relay,
):
    n_dia, n_sub, n_rad, n_y, n_core = sizes
    layers, rows, width = s_v.shape
    full_rows, full = rows + 8, width + 128
    dia, sub, rad, core, z, g, n_z, n_g, along_z, in_plane = places(sizes)
    reach = max(1, n_z // 4)
    own = pl.ds(H, layers)
    near = sorted((k for k in range(1, n_z) if min(k, n_z - k) <= reach), key=lambda k: -min(k, n_z - k))

    has_up, has_down = sub < n_sub - 1, sub > 0
    has_above, has_below = rad < n_rad - 1, rad > 0
    above, below = {"rad": jnp.minimum(rad + 1, n_rad - 1)}, {"rad": jnp.maximum(rad - 1, 0)}
    up, down = {"sub": jnp.minimum(sub + 1, n_sub - 1)}, {"sub": jnp.maximum(sub - 1, 0)}
    right, left = {"dia": lax.rem(dia + 1, n_dia)}, {"dia": lax.rem(dia + n_dia - 1, n_dia)}

    barrier = pltpu.get_barrier_semaphore()
    far_up = jnp.logical_and(core == n_core - 1, has_up)
    far_down = jnp.logical_and(core == 0, has_down)

    @pl.when(far_up)
    def _():
        pl.semaphore_signal(barrier, inc=1, device_id=up, device_id_type=MESH)

    @pl.when(far_down)
    def _():
        pl.semaphore_signal(barrier, inc=1, device_id=down, device_id_type=MESH)

    for k in near:
        pl.semaphore_signal(barrier, inc=1, device_id=along_z(k), device_id_type=MESH)

    loads = [
        pltpu.make_async_copy(s_hbm, s_v, load_sem.at[0]),
        pltpu.make_async_copy(f_hbm, d_v, load_sem.at[1]),
        pltpu.make_async_copy(t_hbm, T.at[own, pl.ds(0, rows), pl.ds(0, width)], load_sem.at[2]),
        pltpu.make_async_copy(m_hbm, m_v, load_sem.at[3]),
    ]
    for copy in loads:
        copy.start()
    for k in range(1, n_g):
        pl.semaphore_signal(barrier, inc=1, device_id=in_plane(k), device_id_type=MESH)
    for copy in loads:
        copy.wait()

    lane = lax.broadcasted_iota(jnp.int32, (1, width), 1)
    picks = [table[i] for i in range(2)]
    choice = jnp.where(lane < width // 2, picks[0], picks[1])

    def motion(c, layer, row=slice(None)):
        return jnp.where(
            choice == 0,
            m_v[0, c, layer].astype(jnp.float32)[row],
            m_v[1, c, layer].astype(jnp.float32)[row],
        )

    def prepare(layer, carry):
        s = s_v[layer]
        diagonal = 6.0 + d_v[layer]
        d_v[layer] = diagonal
        inverse = 1.0 / diagonal
        I[H + layer, :rows, :width] = inverse
        Q[H + layer, :rows, :width] = -0.5 * s * inverse
        v = motion(0, layer)
        eu0[layer + 1] = (0.25 + 0.125 * v) * s
        ed0[layer + 1] = (0.25 - 0.125 * v) * s
        return carry

    lax.fori_loop(0, layers, prepare, 0)

    def row_plan(way):
        if way == 0:
            t, q, i = (rows - 3, rows + 5, 3), (rows - 2, rows + 6, 2), (rows - 1, rows + 7, 1)
            deep = ((T, rows - 4, rows + 4), (Q, rows - 3, rows + 5), (I, rows - 2, rows + 6))
            deeper = range(layers // 2, layers)
        else:
            t, q, i = (0, rows, 3), (0, rows, 2), (0, rows, 1)
            deep = ((T, 3, rows + 3), (Q, 2, rows + 2), (I, 1, rows + 1))
            deeper = range(layers // 2)
        plan = []
        for pair in range(layers // 2):
            plan += [(T, 2 * pair, *t), (T, 2 * pair + 1, *t), (Q, 2 * pair, *q)]
        for pair in range(layers // 2):
            plan.append((Q, 2 * pair + 1, *q))
        plan += [(I, l, *i) for l in range(layers)]
        for l in deeper:
            plan += [(ref, l, src, dst, 1) for ref, src, dst in deep]
        at, placed = 0, []
        for ref, l, src, dst, count in plan:
            placed.append((ref, H + l, src, dst, count, at // 8, at % 8))
            at += count
        return placed

    def pack(columns):
        for way in range(2):
            for ref, L, src, _, count, tile, at in row_plan(way):
                sub_out[way, tile, at : at + count, columns] = ref[L, src : src + count, columns]

    def pack_edges():
        for l in range(layers):
            v = motion(1, l)
            s = s_v[l]
            sub_out[0, layers, l : l + 1, :width] = ((0.25 - 0.125 * v) * s)[rows - 1 : rows]
            sub_out[1, layers, l : l + 1, :width] = ((0.25 + 0.125 * v) * s)[0:1]

    main, side = slice(0, width), slice(width, full)
    pack(main)
    pack_edges()

    tile_lane = lax.broadcasted_iota(jnp.int32, (1, 128), 1)
    packed = [jnp.zeros((8, 128), jnp.float32), jnp.zeros((8, 128), jnp.float32)]
    for l in range(layers):
        for half in range(rows // 8):
            k = l * (rows // 8) + half
            group = slice(8 * half, 8 * half + 8)
            for side_at, at in ((0, slice(width - 128, width)), (1, slice(0, 128))):
                pick = picks[1] if side_at == 0 else picks[0]
                v = jnp.where(
                    pick == 0,
                    m_v[0, 2, l, :, at].astype(jnp.float32)[group],
                    m_v[1, 2, l, :, at].astype(jnp.float32)[group],
                )
                sign = -0.125 if side_at == 0 else 0.125
                e = (0.25 + sign * v) * s_v[l, group, at]
                items = (T[H + l, group, at], Q[H + l, group, at], I[H + l, group, at], e)
                tile = packed[side_at]
                for n, item in enumerate(items):
                    if side_at == 0:
                        low = 124 - 4 * n - 16 * k
                        moved = pltpu.roll(item, (low - 124) % 128, 1)
                    else:
                        low = 4 * n + 16 * k
                        moved = pltpu.roll(item, low % 128, 1)
                    tile = jnp.where((tile_lane >= low) & (tile_lane < low + 4), moved, tile)
                packed[side_at] = tile
    dia_out[0] = packed[0]
    dia_out[1] = packed[1]

    halo_low, halo_high = pl.ds(0, H), pl.ds(H + layers, H)

    @pl.when(jnp.logical_not(has_below))
    def _():
        fwd_in[0] = jnp.zeros(fwd_in.shape[1:], jnp.float32)
        for ref in (T, Q, I):
            ref[halo_low] = jnp.zeros((H, full_rows, full), jnp.float32)
        ed0[0] = jnp.zeros((rows, width), jnp.float32)

    @pl.when(jnp.logical_not(has_above))
    def _():
        fwd_in[1] = jnp.zeros(fwd_in.shape[1:], jnp.float32)
        for ref in (T, Q, I):
            ref[halo_high] = jnp.zeros((H, full_rows, full), jnp.float32)
        eu0[layers + 1] = jnp.zeros((rows, width), jnp.float32)

    @pl.when(jnp.logical_not(has_down))
    def _():
        sub_in[0] = jnp.zeros(sub_in.shape[1:], jnp.float32)
        side_in[0] = jnp.zeros(side_in.shape[1:], jnp.float32)

    @pl.when(jnp.logical_not(has_up))
    def _():
        sub_in[1] = jnp.zeros(sub_in.shape[1:], jnp.float32)
        side_in[1] = jnp.zeros(side_in.shape[1:], jnp.float32)

    pl.semaphore_wait(
        barrier, len(near) + n_g - 1 + far_up.astype(jnp.int32) + far_down.astype(jnp.int32)
    )

    def send(src, dst, ssem, rsem, device):
        return pltpu.make_async_remote_copy(
            src_ref=src, dst_ref=dst, send_sem=ssem, recv_sem=rsem,
            device_id=device, device_id_type=MESH,
        )

    chunks = (pl.ds(0, width // 2), pl.ds(width // 2, width // 2))
    sub_main = [
        [
            send(sub_out.at[i, pl.ds(0, layers), :, at], sub_in.at[i, pl.ds(0, layers), :, at], sub_s.at[i, j], sub_r.at[i, j], to)
            for j, at in enumerate(chunks)
        ]
        for i, to in enumerate((up, down))
    ]
    sub_side = [
        send(side_out.at[i], side_in.at[i], cor_s.at[i], cor_r.at[i], to)
        for i, to in enumerate((up, down))
    ]
    sub_edge = [
        send(sub_out.at[i, layers, :, pl.ds(0, width)], sub_in.at[i, layers, :, pl.ds(0, width)], edge_s.at[i], edge_r.at[i], to)
        for i, to in enumerate((up, down))
    ]
    dia_copies = [
        send(dia_out.at[i], dia_in.at[i], dia_s.at[i], dia_r.at[i], to)
        for i, to in enumerate((right, left))
    ]

    def slab(ref, first, count, rows_at, lanes_at):
        return ref.at[pl.ds(first, count), pl.ds(*rows_at), pl.ds(*lanes_at)]

    def layer_copies(counts, rows_at, lanes_at, ssem, rsem, ahead=0):
        both = [[], []]
        for n, (ref, count) in enumerate(zip((T, Q, I), counts)):
            skip = (3 - n) if ahead else 0
            both[0].append(send(
                slab(ref, H + layers - count - skip, count, rows_at[0], lanes_at),
                slab(ref, H - count - skip, count, rows_at[0], lanes_at),
                ssem.at[0, n], rsem.at[0, n], above,
            ))
            both[1].append(send(
                slab(ref, H + skip, count, rows_at[1], lanes_at),
                slab(ref, H + layers + skip, count, rows_at[1], lanes_at),
                ssem.at[1, n], rsem.at[1, n], below,
            ))
        return both

    all_rows = ((0, rows), (0, rows))
    rad_main = layer_copies((3, 2, 1), all_rows, (0, width), rad_s.at[0], rad_r.at[0])
    rad_deep = layer_copies((1, 1, 1), ((8, 8), (0, 8)), (0, width), rad_s.at[1], rad_r.at[1], 1)
    rad_side = layer_copies((3, 2, 1), all_rows, (width, 128), fwd_s, fwd_r)
    rad_edge = [
        [send(ed0.at[layers], ed0.at[0], edge_s.at[2], edge_r.at[2], above)],
        [send(eu0.at[1], eu0.at[layers + 1], edge_s.at[3], edge_r.at[3], below)],
    ]
    parts = (pl.ds(0, width // 2), pl.ds(width // 2, full - width // 2))
    rad_rows = [
        [
            send(fwd_out.at[i, :, :, at], fwd_in.at[i, :, :, at], late_s.at[i, j], late_r.at[i, j], to)
            for j, at in enumerate(parts)
        ]
        for i, to in enumerate((above, below))
    ]

    def corner_plan(way):
        far = (rows, 1) if way == 0 else (rows + 7, -1)
        near_side = (rows + 7, -1) if way == 0 else (rows, 1)

        def run(side, depth):
            return (side[0] if side[1] > 0 else side[0] - depth + 1, depth)

        plan = [(T, 1, *run(far, 3)), (T, 2, *run(far, 2)), (Q, 1, *run(far, 2)), (T, 3, *run(far, 1))]
        plan += [(T, 1, *run(near_side, 2)), (Q, 2, *run(far, 1)), (I, 1, *run(far, 1))]
        plan += [(T, 2, *run(near_side, 1)), (Q, 1, *run(near_side, 1))]
        at, placed = 0, []
        for ref, depth, first_row, count in plan:
            src = H + layers - depth if way == 0 else H + depth - 1
            dst = H - depth if way == 0 else H + layers + depth - 1
            placed.append((ref, src, dst, first_row, count, at // 8, at % 8))
            at += count
        return placed

    def start(copies, flag):
        @pl.when(flag)
        def _():
            for copy in copies:
                copy.start()

    def arrived(copies, flag):
        @pl.when(flag)
        def _():
            for copy in copies:
                copy.wait_recv()

    def left_here(copies, flag):
        @pl.when(flag)
        def _():
            for copy in copies:
                copy.wait_send()

    for j in range(2):
        start([sub_main[0][j]], has_up)
        start([sub_main[1][j]], has_down)
    for copy in dia_copies:
        copy.start()
    for group in (rad_main, rad_deep):
        start(group[0], has_above)
        start(group[1], has_below)

    for k in sorted({reach, n_z - reach}):
        pl.semaphore_signal(relay, inc=1, device_id=along_z(k), device_id_type=MESH)

    for copy in dia_copies:
        copy.wait_recv()
    for l in range(layers):
        for half in range(rows // 8):
            k = l * (rows // 8) + half
            group = slice(8 * half, 8 * half + 8)
            for n, ref in enumerate((T, Q, I)):
                from_left = pltpu.roll(dia_in[0], (4 * n + 16 * k) % 128, 1)
                from_right = pltpu.roll(dia_in[1], (-4 * n - 16 * k) % 128, 1)
                ref[H + l, group, width:full] = jnp.where(tile_lane < 64, from_right, from_left)
    pack(side)
    for way in range(2):
        tile = sub_out[way, 0, :, side]
        for k in range(1, layers - 1):
            low = 8 * k - 4
            tile = jnp.where((tile_lane >= low) & (tile_lane < low + 8), pltpu.roll(sub_out[way, k, :, side], 8 * k, 1), tile)
        side_out[way] = tile
    start([sub_side[0]], has_up)
    start([sub_side[1]], has_down)
    start(rad_side[0], has_above)
    start(rad_side[1], has_below)
    start([sub_edge[0]], has_up)
    start([sub_edge[1]], has_down)
    start(rad_edge[0], has_above)
    start(rad_edge[1], has_below)

    def unpack(columns):
        for way in range(2):
            for ref, L, _, dst, count, tile, at in row_plan(way):
                ref[L, dst : dst + count, columns] = sub_in[way, tile, at : at + count, columns]

    low_half, high_half, every = slice(0, 8), slice(8, 16), slice(0, full_rows)
    inner, outer = slice(0, rows), slice(rows, full_rows)
    bottom, top = H - 1, H + layers

    def across_layers(L, at):
        z0[0, L, at] = Q[L, at] * (T[L + 1, at] - T[L - 1, at])

    def across_rows(L, at):
        t = T[L]
        z0[1, L, at] = Q[L, at] * (later(t, 0) - earlier(t, 0))[at]

    def across_columns(L, at):
        t = T[L, at]
        z0[2, L, at] = Q[L, at] * (later(t, 1) - earlier(t, 1))

    def column_sum(ref, c, L, at):
        x = ref[c, L, at]
        return later(x, 1) + earlier(x, 1)

    def other_sum(ref, c, L, at):
        x = ref[c, L]
        return ref[c, L + 1, at] + ref[c, L - 1, at] + (later(x, 0) + earlier(x, 0))[at]

    def over_layers(step, beyond, at, deep=True):
        lax.fori_loop(bottom - beyond + 1, top + beyond, lambda L, carry: (step(L, at), carry)[1], 0)
        if deep:
            step(bottom - beyond, high_half)
            step(top + beyond, low_half)

    def forward(columns, j):
        for way in range(2):
            for ref, src, _, row_at, count, tile, at in corner_plan(way):
                fwd_out[way, tile, at : at + count, columns] = ref[src, row_at : row_at + count, columns]
        start([rad_rows[0][j]], has_above)
        start([rad_rows[1][j]], has_below)

    arrived([sub_main[0][0]], has_down)
    arrived([sub_main[1][0]], has_up)
    unpack(slice(0, width // 2))
    forward(slice(0, width // 2), 0)

    for group in (rad_main, rad_deep, rad_side):
        arrived(group[0], has_below)
        arrived(group[1], has_above)

    def early(L, at):
        across_layers(L, at)
        across_rows(L, at)
        across_columns(L, at)

    def early_second(L, at):
        for c in range(3):
            total = column_sum(z0, c, L, at)
            z1[c, L, at] = total
            trial[c, L, at] = I[L, at] * (total + other_sum(z0, c, L, at))

    def early_third(L, at):
        for c in range(3):
            z2[c, L, at] = column_sum(trial, c, L, at)

    over_layers(early, 2, inner)
    over_layers(early_second, 1, inner)
    over_layers(early_third, 0, inner, False)

    octet = lax.broadcasted_iota(jnp.int32, (8, full), 0)

    def late_sums(ref, target, c, L, reach):
        x = ref[c, L]
        up_rows = (octet >= 4 - reach) & (octet < 4)
        down_rows = (octet >= 4) & (octet < 4 + reach)
        tile = jnp.where(up_rows, pltpu.roll(x[8:16], 4, 0), jnp.where(down_rows, pltpu.roll(x[0:8], 4, 0), x[16:24]))
        total = later(tile, 1) + earlier(tile, 1)
        moved = pltpu.roll(total, 4, 0)
        first_tile = jnp.where(octet < reach, moved, target[c, L, 0:8])
        last_tile = jnp.where(octet >= 8 - reach, moved, target[c, L, 8:16])
        return jnp.concatenate([first_tile, last_tile, total], 0)

    arrived([sub_main[0][1]], has_down)
    arrived([sub_main[1][1]], has_up)
    unpack(slice(width // 2, width))
    arrived([sub_side[0]], has_down)
    arrived([sub_side[1]], has_up)
    for way in range(2):
        for k in range(layers - 1):
            sub_in[way, k, :, side] = pltpu.roll(side_in[way], (-8 * k) % 128, 1)
    unpack(side)
    forward(slice(width // 2, full), 1)

    def late(L, carry):
        across_layers(L, outer)
        across_columns(L, outer)
        across_rows(L, every)
        return carry

    lax.fori_loop(H + 1, H + layers - 1, late, 0)
    arrived(rad_rows[0], has_below)
    arrived(rad_rows[1], has_above)
    for way in range(2):
        for ref, _, dst, row_at, count, tile, at in corner_plan(way):
            ref[dst, row_at : row_at + count] = fwd_in[way, tile, at : at + count]

    lax.fori_loop(bottom - 1, H + 1, late, 0)
    lax.fori_loop(H + layers - 1, top + 2, late, 0)
    across_rows(bottom - 2, high_half)
    across_rows(top + 2, low_half)

    def second(L, carry):
        for c in range(3):
            z1[c, L] = I[L] * (late_sums(z0, z1, c, L, 1) + other_sum(z0, c, L, every))
        return carry

    def second_deep(L, at):
        for c in (0, 2):
            z1[c, L, at] = I[L, at] * (z1[c, L, at] + other_sum(z0, c, L, at))
        z1[1, L, at] = I[L, at] * (column_sum(z0, 1, L, at) + other_sum(z0, 1, L, at))

    def third(L, carry):
        for c in range(3):
            z2[c, L] = I[L] * (late_sums(z1, z2, c, L, 2) + other_sum(z1, c, L, every))
        return carry

    def third_deep(L, at):
        for c in range(3):
            z2[c, L, at] = I[L, at] * (column_sum(z1, c, L, at) + other_sum(z1, c, L, at))

    lax.fori_loop(bottom, top + 1, second, 0)
    second_deep(bottom - 1, high_half)
    second_deep(top + 1, low_half)
    lax.fori_loop(H, H + layers, third, 0)
    third_deep(bottom, high_half)
    third_deep(top, low_half)

    def folded(x):
        total = jnp.zeros((8, 128), jnp.float32)
        for r in range(0, rows, 8):
            for w in range(0, width, 128):
                total = total + x[r : r + 8, w : w + 128]
        return total

    row_at = lax.broadcasted_iota(jnp.int32, (rows, width), 0)

    def moments(l, sums):
        L = H + l
        d = d_v[l]
        new = [0.0] * 6
        for c in range(3):
            a, b, e = z0[c, L, :rows, :width], z1[c, L, :rows, :width], z2[c, L, :rows, :width]
            x = z2[c, L]
            ahead = jnp.where((row_at < 8) | (l < layers - 1), z2[c, L + 1, :rows, :width], 0.0)
            ahead += jnp.where((row_at < rows - 1) | (l < layers // 2), later(x, 0)[:rows, :width], 0.0)
            ahead += jnp.where((row_at == 0) & (l >= layers // 2), earlier(x, 0)[:rows, :width], 0.0)
            ahead += later(x[:rows], 1)[:, :width]
            da, db, de = d * a, d * b, d * e
            for j, term in enumerate((da * a, da * b, db * b, db * e, de * e, e * ahead)):
                new[j] = new[j] + term
        return tuple(total + folded(x) for total, x in zip(sums, new))

    sums = list(lax.fori_loop(0, layers, moments, (jnp.zeros((8, 128), jnp.float32),) * 6))
    for c in range(3):
        joint = z2[c, H, high_half, :width] * z2[c, bottom, high_half, :width]
        for w in range(0, width, 128):
            sums[5] = sums[5] + joint[:, w : w + 128]
    sums[5] = 2.0 * sums[5]

    row = jnp.zeros((1, 128), jnp.float32)
    for j in range(6):
        row = jnp.where(tile_lane == j, jnp.sum(sums[j], keepdims=True), row)

    def exchange(value, turn, slots, count, index, peer, ssem, rsem, order):
        mine[turn] = value
        slots[index] = value
        for k in order:
            send(mine.at[turn], slots.at[index], ssem, rsem, peer(k)).start()
        return send(slots.at[pl.ds(0, count - 1)], slots.at[pl.ds(0, count - 1)], ssem, rsem, peer(1))

    def hops(k):
        across, along = k // (n_y * n_core), (k // n_core) % n_y
        return min(across, n_rad - across) + min(along, n_y - along)

    far_in_plane = sorted(range(1, n_g), key=lambda k: -hops(k))
    in_plane_copies = exchange(row, 0, plane, n_g, g, in_plane, plane_s, plane_r, far_in_plane)
    stores = [
        pltpu.make_async_copy(ref.at[:, own, pl.ds(0, rows), pl.ds(0, width)], zs_hbm.at[k], store_sem.at[k])
        for k, ref in enumerate((z0, z1, z2))
    ]
    in_plane_copies.wait_recv()
    row = jnp.sum(plane[...], axis=0)
    far_first = sorted(range(1, n_z), key=lambda k: -min(k, n_z - k))
    pl.semaphore_wait(relay, len({reach, n_z - reach}))
    copies = exchange(row, 1, column, n_z, z, along_z, column_s, column_r, far_first)

    for copy in stores:
        copy.start()
    arrived([sub_edge[0]], has_down)
    arrived([sub_edge[1]], has_up)
    arrived(rad_edge[0], has_below)
    arrived(rad_edge[1], has_above)

    def advect(l, carry):
        s = s_v[l]
        v1, v2 = motion(1, l), motion(2, l)
        total = -0.5 * s + eu0[l + 2] + ed0[l]
        u, w = (0.25 + 0.125 * v1) * s, (0.25 - 0.125 * v1) * s
        total = total + jnp.where(row_at == rows - 1, sub_in[1, layers, pl.ds(l, 1), :width], later(u, 0))
        total = total + jnp.where(row_at == 0, sub_in[0, layers, pl.ds(l, 1), :width], earlier(w, 0))
        u, w = (0.25 + 0.125 * v2) * s, (0.25 - 0.125 * v2) * s
        temp_v[l] = total + later(u, 1) + earlier(w, 1)
        return carry

    lax.fori_loop(0, layers, advect, 0)
    for l in range(layers):
        for half in range(rows // 8):
            k = l * (rows // 8) + half
            group = slice(8 * half, 8 * half + 8)
            s_low, s_high = s_v[l, group, 0:128], s_v[l, group, width - 128 : width]

            def speed(at, pick, group=group, l=l):
                return jnp.where(
                    pick == 0,
                    m_v[0, 2, l, :, at].astype(jnp.float32)[group],
                    m_v[1, 2, l, :, at].astype(jnp.float32)[group],
                )

            low, high = slice(0, 128), slice(width - 128, width)
            u = pltpu.roll((0.25 + 0.125 * speed(low, picks[0])) * s_low, 127, 1)
            w = pltpu.roll((0.25 - 0.125 * speed(high, picks[1])) * s_high, 1, 1)
            from_left = pltpu.roll(dia_in[0], (13 + 16 * k) % 128, 1)
            from_right = pltpu.roll(dia_in[1], (127 - 12 - 16 * k) % 128, 1)
            temp_v[l, group, low] += jnp.where(tile_lane == 0, from_left - w, 0.0)
            temp_v[l, group, high] += jnp.where(tile_lane == 127, from_right - u, 0.0)

    stores.append(pltpu.make_async_copy(temp_v, adv_hbm, store_sem.at[3]))
    stores[3].start()
    left_here(sub_main[0] + [sub_side[0], sub_edge[0]], has_up)
    left_here(sub_main[1] + [sub_side[1], sub_edge[1]], has_down)
    for copy in dia_copies:
        copy.wait_send()
    for group in (rad_main, rad_deep, rad_side, rad_rows, rad_edge):
        left_here(group[0], has_above)
        left_here(group[1], has_below)
    for copy in stores:
        copy.wait()
    in_plane_copies.wait_send()

    copies.wait_recv()
    copies.wait_send()
    row = jnp.sum(column[...], axis=0)
    m0, m1, m2, m3, m4, m5 = (
        jnp.sum(jnp.where(tile_lane == j, row, 0.0), axis=1, keepdims=True) for j in range(6)
    )

    def step(p):
        a, b, c = p
        square = (a * a, 2.0 * a * b, b * b + 2.0 * a * c, 2.0 * b * c, c * c)
        energy = sum(x * m for x, m in zip(square, (m0, m1, m2, m3, m4)))
        moved = sum(x * m for x, m in zip(square, (m1, m2, m3, m4, m5)))
        return jnp.clip(energy / (energy - moved), ALPHA_LOW, ALPHA_HIGH)

    one, none = jnp.ones_like(m0), jnp.zeros_like(m0)
    p0 = (one, none, none)
    alpha0 = step(p0)
    p1 = (1.0 - alpha0, alpha0, none)
    alpha1 = step(p1)
    p2 = (p1[0] * (1.0 - alpha1), p1[1] * (1.0 - alpha1) + p1[0] * alpha1, p1[1] * alpha1)
    alpha2 = step(p2)
    c0, c1, c2 = (alpha0 * x + alpha1 * y + alpha2 * w for x, y, w in zip(p0, p1, p2))

    wide = jnp.zeros((8, 128), jnp.float32)
    row_of = lax.broadcasted_iota(jnp.int32, (8, 128), 0)
    for n, value in enumerate((c0, c1, c2)):
        wide = jnp.where(row_of == n, value, wide)
    coef_ref[...] = wide


def finish(coef_hbm, adv_hbm, zs_hbm, temp_hbm, vel_hbm, coef, adv, zs, temp, vel, load_sem, store_sem):
    layers = adv.shape[0]
    loads, stores = [pltpu.make_async_copy(coef_hbm, coef, load_sem.at[2, 0])], []
    loads[0].start()
    for l in range(layers):
        loads.append(pltpu.make_async_copy(zs_hbm.at[:, :, l], zs.at[:, :, l], load_sem.at[0, l]))
        loads.append(pltpu.make_async_copy(adv_hbm.at[l], adv.at[l], load_sem.at[1, l]))
        stores.append(pltpu.make_async_copy(vel.at[:, l], vel_hbm.at[:, l], store_sem.at[0, l]))
        stores.append(pltpu.make_async_copy(temp.at[l], temp_hbm.at[l], store_sem.at[1, l]))
        loads[-2].start()
        loads[-1].start()
    loads[0].wait()
    c0, c1, c2 = (coef[n : n + 1, 0:1] for n in range(3))
    for l in range(layers):
        loads[2 * l + 1].wait()
        loads[2 * l + 2].wait()
        for c in range(3):
            velocity = c0 * zs[0, c, l] + c1 * zs[1, c, l] + c2 * zs[2, c, l]
            vel[c, l] = velocity
            if c == 0:
                temp[l] = adv[l] + 4.0 * velocity
        stores[2 * l].start()
        stores[2 * l + 1].start()
    for copy in stores:
        copy.wait()


def solution(mesh):
    shape = mesh.shape
    n_y = Y_COUNT if shape["sub"] >= 32 else 1
    sizes = (shape["dia"], shape["sub"], shape["rad"], n_y, CORES)
    n_z = shape["dia"] * shape["sub"] // (n_y * CORES)
    n_g = shape["rad"] * n_y * CORES

    def shards(sensitivity_heat, stored_heat, friction_diagonal, stored_motions, record_choice_table):
        layers, rows, width = sensitivity_heat.shape
        tall, wide, long = layers + 2 * H, rows + 8, width + 128
        f32 = jnp.float32
        block = pltpu.VMEM((layers, rows, width), f32)
        field = pltpu.VMEM((tall, wide, long), f32)
        vector = pltpu.VMEM((3, tall, wide, long), f32)
        dma = pltpu.SemaphoreType.DMA
        in_hbm = pl.BlockSpec(memory_space=pltpu.HBM)
        advected, zs, coefficients = pl.pallas_call(
            functools.partial(kernel, sizes),
            out_shape=(
                jax.ShapeDtypeStruct((layers, rows, width), f32),
                jax.ShapeDtypeStruct((3, 3, layers, rows, width), f32),
                jax.ShapeDtypeStruct((8, 128), f32),
            ),
            in_specs=[pl.BlockSpec(memory_space=pltpu.SMEM)] + [in_hbm] * 4,
            out_specs=(in_hbm, in_hbm, pl.BlockSpec(memory_space=pltpu.VMEM)),
            scratch_shapes=[
                block, block, pltpu.VMEM(stored_motions.shape, stored_motions.dtype),
                field, field, field, vector, vector, vector, vector,
                pltpu.VMEM((layers + 2, rows, width), f32), pltpu.VMEM((layers + 2, rows, width), f32),
                pltpu.VMEM((2, layers + 1, 8, long), f32), pltpu.VMEM((2, layers + 1, 8, long), f32),
                pltpu.VMEM((2, 8, 128), f32), pltpu.VMEM((2, 8, 128), f32),
                pltpu.VMEM((2, 2, 8, long), f32), pltpu.VMEM((2, 2, 8, long), f32),
                pltpu.VMEM((2, 8, 128), f32), pltpu.VMEM((2, 8, 128), f32), pltpu.VMEM((2, 1, 128), f32), pltpu.VMEM((n_g, 1, 128), f32), pltpu.VMEM((n_z, 1, 128), f32),
                block,
                dma((4,)), dma((4,)), dma((2,)), dma((2,)), dma((2, 2, 3)), dma((2, 2, 3)),
                dma((2, 2)), dma((2, 2)), dma((2,)), dma((2,)), dma((2, 3)), dma((2, 3)),
                dma((2, 2)), dma((2, 2)), dma((4,)), dma((4,)),
                dma, dma, dma, dma, pltpu.SemaphoreType.REGULAR,
            ],
            compiler_params=pltpu.CompilerParams(
                collective_id=0, has_side_effects=True, vmem_limit_bytes=60 * 2**20
            ),
            name="adjoint_step",
        )(record_choice_table, sensitivity_heat, stored_heat, friction_diagonal, stored_motions)
        return pl.pallas_call(
            finish,
            out_shape=(
                jax.ShapeDtypeStruct((layers, rows, width), f32),
                jax.ShapeDtypeStruct((3, layers, rows, width), f32),
            ),
            in_specs=[in_hbm] * 3,
            out_specs=(in_hbm, in_hbm),
            scratch_shapes=[
                pltpu.VMEM((8, 128), f32), block, pltpu.VMEM((3, 3, layers, rows, width), f32),
                block, pltpu.VMEM((3, layers, rows, width), f32), dma((3, layers)), dma((2, layers)),
            ],
            compiler_params=pltpu.CompilerParams(vmem_limit_bytes=60 * 2**20),
            name="finish",
        )(coefficients, advected, zs)

    placed = (
        P("rad", "sub", "dia"),
        P("rad", "sub", "dia"),
        P("rad", "sub", "dia"),
        P(None, None, "rad", "sub", "dia"),
        P("dia"),
    )
    return jax.shard_map(
        shards,
        mesh=mesh,
        in_specs=placed,
        out_specs=(P("rad", "sub", "dia"), P(None, "rad", "sub", "dia")),
        check_vma=False,
    )
```

```python
import functools

import jax
import jax.numpy as jnp
from jax import lax
from jax.experimental import pallas as pl
from jax.experimental.pallas import tpu as pltpu
from jax.sharding import PartitionSpec as P

MESH = pl.DeviceIdType.MESH
H = 4
Y_COUNT, CORES = 4, 2
ALPHA_LOW, ALPHA_HIGH = 0.5, 62.0


def later(x, axis):
    return pltpu.roll(x, x.shape[axis] - 1, axis)


def earlier(x, axis):
    return pltpu.roll(x, 1, axis)


def places(sizes):
    n_dia, n_sub, n_rad, n_y, n_core = sizes
    n_zh = n_sub // (n_y * n_core)
    dia, sub, rad = lax.axis_index("dia"), lax.axis_index("sub"), lax.axis_index("rad")
    y, zh, core = sub // (n_zh * n_core), (sub // n_core) % n_zh, sub % n_core
    n_z = n_zh * n_dia
    n_g = n_rad * n_y * n_core
    z = zh * n_dia + dia
    g = (rad * n_y + y) * n_core + core

    def along_z(k):
        t = lax.rem(z + k, n_z)
        return {"sub": (y * n_zh + t // n_dia) * n_core + core, "dia": t % n_dia}

    def in_plane(k):
        t = lax.rem(g + k, n_g)
        r2, y2, c2 = t // (n_y * n_core), (t // n_core) % n_y, t % n_core
        return {"sub": (y2 * n_zh + zh) * n_core + c2, "rad": r2}

    return dia, sub, rad, core, z, g, n_z, n_g, along_z, in_plane


def kernel(
    sizes, table, s_hbm, t_hbm, f_hbm, m_hbm, adv_hbm, zs_hbm, coef_ref,
    s_v, d_v, m_v, T, Q, I, z0, z1, z2, trial, eu0, ed0,
    sub_out, sub_in, dia_out, dia_in, fwd_out, fwd_in, side_out, side_in, mine, plane, column, temp_v,
    load_sem, store_sem, dia_s, dia_r, rad_s, rad_r, sub_s, sub_r, cor_s, cor_r, fwd_s, fwd_r, late_s, late_r, edge_s, edge_r,
    plane_s, plane_r, column_s, column_r, relay,
):
    n_dia, n_sub, n_rad, n_y, n_core = sizes
    layers, rows, width = s_v.shape
    full_rows, full = rows + 8, width + 128
    dia, sub, rad, core, z, g, n_z, n_g, along_z, in_plane = places(sizes)
    reach = max(1, n_z // 4)
    own = pl.ds(H, layers)
    near = sorted((k for k in range(1, n_z) if min(k, n_z - k) <= reach), key=lambda k: -min(k, n_z - k))

    has_up, has_down = sub < n_sub - 1, sub > 0
    has_above, has_below = rad < n_rad - 1, rad > 0
    above, below = {"rad": jnp.minimum(rad + 1, n_rad - 1)}, {"rad": jnp.maximum(rad - 1, 0)}
    up, down = {"sub": jnp.minimum(sub + 1, n_sub - 1)}, {"sub": jnp.maximum(sub - 1, 0)}
    right, left = {"dia": lax.rem(dia + 1, n_dia)}, {"dia": lax.rem(dia + n_dia - 1, n_dia)}

    barrier = pltpu.get_barrier_semaphore()
    far_up = jnp.logical_and(core == n_core - 1, has_up)
    far_down = jnp.logical_and(core == 0, has_down)

    @pl.when(far_up)
    def _():
        pl.semaphore_signal(barrier, inc=1, device_id=up, device_id_type=MESH)

    @pl.when(far_down)
    def _():
        pl.semaphore_signal(barrier, inc=1, device_id=down, device_id_type=MESH)

    for k in near:
        pl.semaphore_signal(barrier, inc=1, device_id=along_z(k), device_id_type=MESH)

    loads = [
        pltpu.make_async_copy(s_hbm, s_v, load_sem.at[0]),
        pltpu.make_async_copy(f_hbm, d_v, load_sem.at[1]),
        pltpu.make_async_copy(t_hbm, T.at[own, pl.ds(0, rows), pl.ds(0, width)], load_sem.at[2]),
        pltpu.make_async_copy(m_hbm, m_v, load_sem.at[3]),
    ]
    for copy in loads:
        copy.start()
    for k in range(1, n_g):
        pl.semaphore_signal(barrier, inc=1, device_id=in_plane(k), device_id_type=MESH)
    for copy in loads:
        copy.wait()

    lane = lax.broadcasted_iota(jnp.int32, (1, width), 1)
    picks = [table[i] for i in range(2)]
    choice = jnp.where(lane < width // 2, picks[0], picks[1])

    def motion(c, layer, row=slice(None)):
        return jnp.where(
            choice == 0,
            m_v[0, c, layer].astype(jnp.float32)[row],
            m_v[1, c, layer].astype(jnp.float32)[row],
        )

    def prepare(layer, carry):
        s = s_v[layer]
        diagonal = 6.0 + d_v[layer]
        d_v[layer] = diagonal
        inverse = 1.0 / diagonal
        I[H + layer, :rows, :width] = inverse
        Q[H + layer, :rows, :width] = -0.5 * s * inverse
        v = motion(0, layer)
        eu0[layer + 1] = (0.25 + 0.125 * v) * s
        ed0[layer + 1] = (0.25 - 0.125 * v) * s
        return carry

    lax.fori_loop(0, layers, prepare, 0)

    def row_plan(way):
        if way == 0:
            t, q, i = (rows - 3, rows + 5, 3), (rows - 2, rows + 6, 2), (rows - 1, rows + 7, 1)
            deep = ((T, rows - 4, rows + 4), (Q, rows - 3, rows + 5), (I, rows - 2, rows + 6))
            deeper = range(layers // 2, layers)
        else:
            t, q, i = (0, rows, 3), (0, rows, 2), (0, rows, 1)
            deep = ((T, 3, rows + 3), (Q, 2, rows + 2), (I, 1, rows + 1))
            deeper = range(layers // 2)
        plan = []
        for pair in range(layers // 2):
            plan += [(T, 2 * pair, *t), (T, 2 * pair + 1, *t), (Q, 2 * pair, *q)]
        for pair in range(layers // 2):
            plan.append((Q, 2 * pair + 1, *q))
        plan += [(I, l, *i) for l in range(layers)]
        for l in deeper:
            plan += [(ref, l, src, dst, 1) for ref, src, dst in deep]
        at, placed = 0, []
        for ref, l, src, dst, count in plan:
            placed.append((ref, H + l, src, dst, count, at // 8, at % 8))
            at += count
        return placed

    def pack(columns):
        for way in range(2):
            for ref, L, src, _, count, tile, at in row_plan(way):
                sub_out[way, tile, at : at + count, columns] = ref[L, src : src + count, columns]

    def pack_edges():
        for l in range(layers):
            v = motion(1, l)
            s = s_v[l]
            sub_out[0, layers, l : l + 1, :width] = ((0.25 - 0.125 * v) * s)[rows - 1 : rows]
            sub_out[1, layers, l : l + 1, :width] = ((0.25 + 0.125 * v) * s)[0:1]

    main, side = slice(0, width), slice(width, full)
    pack(main)
    pack_edges()

    tile_lane = lax.broadcasted_iota(jnp.int32, (1, 128), 1)
    packed = [jnp.zeros((8, 128), jnp.float32), jnp.zeros((8, 128), jnp.float32)]
    for l in range(layers):
        for half in range(rows // 8):
            k = l * (rows // 8) + half
            group = slice(8 * half, 8 * half + 8)
            for side_at, at in ((0, slice(width - 128, width)), (1, slice(0, 128))):
                pick = picks[1] if side_at == 0 else picks[0]
                v = jnp.where(
                    pick == 0,
                    m_v[0, 2, l, :, at].astype(jnp.float32)[group],
                    m_v[1, 2, l, :, at].astype(jnp.float32)[group],
                )
                sign = -0.125 if side_at == 0 else 0.125
                e = (0.25 + sign * v) * s_v[l, group, at]
                items = (T[H + l, group, at], Q[H + l, group, at], I[H + l, group, at], e)
                tile = packed[side_at]
                for n, item in enumerate(items):
                    if side_at == 0:
                        low = 124 - 4 * n - 16 * k
                        moved = pltpu.roll(item, (low - 124) % 128, 1)
                    else:
                        low = 4 * n + 16 * k
                        moved = pltpu.roll(item, low % 128, 1)
                    tile = jnp.where((tile_lane >= low) & (tile_lane < low + 4), moved, tile)
                packed[side_at] = tile
    dia_out[0] = packed[0]
    dia_out[1] = packed[1]

    halo_low, halo_high = pl.ds(0, H), pl.ds(H + layers, H)

    @pl.when(jnp.logical_not(has_below))
    def _():
        fwd_in[0] = jnp.zeros(fwd_in.shape[1:], jnp.float32)
        for ref in (T, Q, I):
            ref[halo_low] = jnp.zeros((H, full_rows, full), jnp.float32)
        ed0[0] = jnp.zeros((rows, width), jnp.float32)

    @pl.when(jnp.logical_not(has_above))
    def _():
        fwd_in[1] = jnp.zeros(fwd_in.shape[1:], jnp.float32)
        for ref in (T, Q, I):
            ref[halo_high] = jnp.zeros((H, full_rows, full), jnp.float32)
        eu0[layers + 1] = jnp.zeros((rows, width), jnp.float32)

    @pl.when(jnp.logical_not(has_down))
    def _():
        sub_in[0] = jnp.zeros(sub_in.shape[1:], jnp.float32)
        side_in[0] = jnp.zeros(side_in.shape[1:], jnp.float32)

    @pl.when(jnp.logical_not(has_up))
    def _():
        sub_in[1] = jnp.zeros(sub_in.shape[1:], jnp.float32)
        side_in[1] = jnp.zeros(side_in.shape[1:], jnp.float32)

    pl.semaphore_wait(
        barrier, len(near) + n_g - 1 + far_up.astype(jnp.int32) + far_down.astype(jnp.int32)
    )

    def send(src, dst, ssem, rsem, device):
        return pltpu.make_async_remote_copy(
            src_ref=src, dst_ref=dst, send_sem=ssem, recv_sem=rsem,
            device_id=device, device_id_type=MESH,
        )

    n_chunks = 4 if width % 512 == 0 else 2
    wide = width // n_chunks
    chunks = [pl.ds(j * wide, wide) for j in range(n_chunks)]
    sub_main = [
        [
            send(sub_out.at[i, pl.ds(0, layers), :, at], sub_in.at[i, pl.ds(0, layers), :, at], sub_s.at[i, j], sub_r.at[i, j], to)
            for j, at in enumerate(chunks)
        ]
        for i, to in enumerate((up, down))
    ]
    sub_side = [
        send(side_out.at[i], side_in.at[i], cor_s.at[i], cor_r.at[i], to)
        for i, to in enumerate((up, down))
    ]
    sub_edge = [
        send(sub_out.at[i, layers, :, pl.ds(0, width)], sub_in.at[i, layers, :, pl.ds(0, width)], edge_s.at[i], edge_r.at[i], to)
        for i, to in enumerate((up, down))
    ]
    dia_copies = [
        send(dia_out.at[i], dia_in.at[i], dia_s.at[i], dia_r.at[i], to)
        for i, to in enumerate((right, left))
    ]

    def slab(ref, first, count, rows_at, lanes_at):
        return ref.at[pl.ds(first, count), pl.ds(*rows_at), pl.ds(*lanes_at)]

    def layer_copies(counts, rows_at, lanes_at, ssem, rsem, ahead=0):
        both = [[], []]
        for n, (ref, count) in enumerate(zip((T, Q, I), counts)):
            skip = (3 - n) if ahead else 0
            both[0].append(send(
                slab(ref, H + layers - count - skip, count, rows_at[0], lanes_at),
                slab(ref, H - count - skip, count, rows_at[0], lanes_at),
                ssem.at[0, n], rsem.at[0, n], above,
            ))
            both[1].append(send(
                slab(ref, H + skip, count, rows_at[1], lanes_at),
                slab(ref, H + layers + skip, count, rows_at[1], lanes_at),
                ssem.at[1, n], rsem.at[1, n], below,
            ))
        return both

    all_rows = ((0, rows), (0, rows))
    rad_main = layer_copies((3, 2, 1), all_rows, (0, width), rad_s.at[0], rad_r.at[0])
    rad_deep = layer_copies((1, 1, 1), ((8, 8), (0, 8)), (0, width), rad_s.at[1], rad_r.at[1], 1)
    rad_side = layer_copies((3, 2, 1), all_rows, (width, 128), fwd_s, fwd_r)
    rad_edge = [
        [send(ed0.at[layers], ed0.at[0], edge_s.at[2], edge_r.at[2], above)],
        [send(eu0.at[1], eu0.at[layers + 1], edge_s.at[3], edge_r.at[3], below)],
    ]
    parts = chunks[:-1] + [pl.ds(width - wide, wide + 128)]
    rad_rows = [
        [
            send(fwd_out.at[i, :, :, at], fwd_in.at[i, :, :, at], late_s.at[i, j], late_r.at[i, j], to)
            for j, at in enumerate(parts)
        ]
        for i, to in enumerate((above, below))
    ]

    def corner_plan(way):
        far = (rows, 1) if way == 0 else (rows + 7, -1)
        near_side = (rows + 7, -1) if way == 0 else (rows, 1)

        def run(side, depth):
            return (side[0] if side[1] > 0 else side[0] - depth + 1, depth)

        plan = [(T, 1, *run(far, 3)), (T, 2, *run(far, 2)), (Q, 1, *run(far, 2)), (T, 3, *run(far, 1))]
        plan += [(T, 1, *run(near_side, 2)), (Q, 2, *run(far, 1)), (I, 1, *run(far, 1))]
        plan += [(T, 2, *run(near_side, 1)), (Q, 1, *run(near_side, 1))]
        at, placed = 0, []
        for ref, depth, first_row, count in plan:
            src = H + layers - depth if way == 0 else H + depth - 1
            dst = H - depth if way == 0 else H + layers + depth - 1
            placed.append((ref, src, dst, first_row, count, at // 8, at % 8))
            at += count
        return placed

    def start(copies, flag):
        @pl.when(flag)
        def _():
            for copy in copies:
                copy.start()

    def arrived(copies, flag):
        @pl.when(flag)
        def _():
            for copy in copies:
                copy.wait_recv()

    def left_here(copies, flag):
        @pl.when(flag)
        def _():
            for copy in copies:
                copy.wait_send()

    for j in range(n_chunks):
        start([sub_main[0][j]], has_up)
        start([sub_main[1][j]], has_down)
    for copy in dia_copies:
        copy.start()
    for group in (rad_main, rad_deep):
        start(group[0], has_above)
        start(group[1], has_below)

    for k in sorted({reach, n_z - reach}):
        pl.semaphore_signal(relay, inc=1, device_id=along_z(k), device_id_type=MESH)

    for copy in dia_copies:
        copy.wait_recv()
    for l in range(layers):
        for half in range(rows // 8):
            k = l * (rows // 8) + half
            group = slice(8 * half, 8 * half + 8)
            for n, ref in enumerate((T, Q, I)):
                from_left = pltpu.roll(dia_in[0], (4 * n + 16 * k) % 128, 1)
                from_right = pltpu.roll(dia_in[1], (-4 * n - 16 * k) % 128, 1)
                ref[H + l, group, width:full] = jnp.where(tile_lane < 64, from_right, from_left)
    pack(side)
    for way in range(2):
        tile = sub_out[way, 0, :, side]
        for k in range(1, layers - 1):
            low = 8 * k - 4
            tile = jnp.where((tile_lane >= low) & (tile_lane < low + 8), pltpu.roll(sub_out[way, k, :, side], 8 * k, 1), tile)
        side_out[way] = tile
    start([sub_side[0]], has_up)
    start([sub_side[1]], has_down)
    start(rad_side[0], has_above)
    start(rad_side[1], has_below)
    start([sub_edge[0]], has_up)
    start([sub_edge[1]], has_down)
    start(rad_edge[0], has_above)
    start(rad_edge[1], has_below)

    def unpack(columns):
        for way in range(2):
            for ref, L, _, dst, count, tile, at in row_plan(way):
                ref[L, dst : dst + count, columns] = sub_in[way, tile, at : at + count, columns]

    low_half, high_half, every = slice(0, 8), slice(8, 16), slice(0, full_rows)
    inner, outer = slice(0, rows), slice(rows, full_rows)
    bottom, top = H - 1, H + layers

    def across_layers(L, at):
        z0[0, L, at] = Q[L, at] * (T[L + 1, at] - T[L - 1, at])

    def across_rows(L, at):
        t = T[L]
        z0[1, L, at] = Q[L, at] * (later(t, 0) - earlier(t, 0))[at]

    def across_columns(L, at):
        t = T[L, at]
        z0[2, L, at] = Q[L, at] * (later(t, 1) - earlier(t, 1))

    def column_sum(ref, c, L, at):
        x = ref[c, L, at]
        return later(x, 1) + earlier(x, 1)

    def other_sum(ref, c, L, at):
        x = ref[c, L]
        return ref[c, L + 1, at] + ref[c, L - 1, at] + (later(x, 0) + earlier(x, 0))[at]

    def over_layers(step, beyond, at, deep=True):
        lax.fori_loop(bottom - beyond + 1, top + beyond, lambda L, carry: (step(L, at), carry)[1], 0)
        if deep:
            step(bottom - beyond, high_half)
            step(top + beyond, low_half)

    def forward(columns, j):
        for way in range(2):
            for ref, src, _, row_at, count, tile, at in corner_plan(way):
                fwd_out[way, tile, at : at + count, columns] = ref[src, row_at : row_at + count, columns]
        start([rad_rows[0][j]], has_above)
        start([rad_rows[1][j]], has_below)

    def take(j, forwarded=True):
        columns = slice(j * wide, (j + 1) * wide)
        arrived([sub_main[0][j]], has_down)
        arrived([sub_main[1][j]], has_up)
        unpack(columns)
        if forwarded:
            forward(columns, j)

    for j in range(n_chunks // 2):
        take(j)

    for group in (rad_main, rad_deep, rad_side):
        arrived(group[0], has_below)
        arrived(group[1], has_above)

    def early(L, at):
        across_layers(L, at)
        across_rows(L, at)
        across_columns(L, at)

    def early_second(L, at):
        for c in range(3):
            total = column_sum(z0, c, L, at)
            z1[c, L, at] = total
            trial[c, L, at] = I[L, at] * (total + other_sum(z0, c, L, at))

    def early_third(L, at):
        for c in range(3):
            z2[c, L, at] = column_sum(trial, c, L, at)

    over_layers(early, 2, inner)
    over_layers(early_second, 1, inner)
    over_layers(early_third, 0, inner, False)

    octet = lax.broadcasted_iota(jnp.int32, (8, full), 0)

    def late_sums(ref, target, c, L, reach):
        x = ref[c, L]
        up_rows = (octet >= 4 - reach) & (octet < 4)
        down_rows = (octet >= 4) & (octet < 4 + reach)
        tile = jnp.where(up_rows, pltpu.roll(x[8:16], 4, 0), jnp.where(down_rows, pltpu.roll(x[0:8], 4, 0), x[16:24]))
        total = later(tile, 1) + earlier(tile, 1)
        moved = pltpu.roll(total, 4, 0)
        first_tile = jnp.where(octet < reach, moved, target[c, L, 0:8])
        last_tile = jnp.where(octet >= 8 - reach, moved, target[c, L, 8:16])
        return jnp.concatenate([first_tile, last_tile, total], 0)

    for j in range(n_chunks // 2, n_chunks):
        take(j, j < n_chunks - 1)
    arrived([sub_side[0]], has_down)
    arrived([sub_side[1]], has_up)
    for way in range(2):
        for k in range(layers - 1):
            sub_in[way, k, :, side] = pltpu.roll(side_in[way], (-8 * k) % 128, 1)
    unpack(side)
    forward(slice(width - wide, full), n_chunks - 1)

    def late(L, carry):
        across_layers(L, outer)
        across_columns(L, outer)
        across_rows(L, every)
        return carry

    lax.fori_loop(H + 1, H + layers - 1, late, 0)
    arrived(rad_rows[0], has_below)
    arrived(rad_rows[1], has_above)
    for way in range(2):
        for ref, _, dst, row_at, count, tile, at in corner_plan(way):
            ref[dst, row_at : row_at + count] = fwd_in[way, tile, at : at + count]

    lax.fori_loop(bottom - 1, H + 1, late, 0)
    lax.fori_loop(H + layers - 1, top + 2, late, 0)
    across_rows(bottom - 2, high_half)
    across_rows(top + 2, low_half)

    def second(L, carry):
        for c in range(3):
            z1[c, L] = I[L] * (late_sums(z0, z1, c, L, 1) + other_sum(z0, c, L, every))
        return carry

    def second_deep(L, at):
        for c in (0, 2):
            z1[c, L, at] = I[L, at] * (z1[c, L, at] + other_sum(z0, c, L, at))
        z1[1, L, at] = I[L, at] * (column_sum(z0, 1, L, at) + other_sum(z0, 1, L, at))

    def third(L, carry):
        for c in range(3):
            z2[c, L] = I[L] * (late_sums(z1, z2, c, L, 2) + other_sum(z1, c, L, every))
        return carry

    def third_deep(L, at):
        for c in range(3):
            z2[c, L, at] = I[L, at] * (column_sum(z1, c, L, at) + other_sum(z1, c, L, at))

    lax.fori_loop(bottom, top + 1, second, 0)
    second_deep(bottom - 1, high_half)
    second_deep(top + 1, low_half)
    lax.fori_loop(H, H + layers, third, 0)
    third_deep(bottom, high_half)
    third_deep(top, low_half)

    def folded(x):
        total = jnp.zeros((8, 128), jnp.float32)
        for r in range(0, rows, 8):
            for w in range(0, width, 128):
                total = total + x[r : r + 8, w : w + 128]
        return total

    row_at = lax.broadcasted_iota(jnp.int32, (rows, width), 0)

    def moments(l, sums):
        L = H + l
        d = d_v[l]
        new = [0.0] * 6
        for c in range(3):
            a, b, e = z0[c, L, :rows, :width], z1[c, L, :rows, :width], z2[c, L, :rows, :width]
            x = z2[c, L]
            ahead = jnp.where((row_at < 8) | (l < layers - 1), z2[c, L + 1, :rows, :width], 0.0)
            ahead += jnp.where((row_at < rows - 1) | (l < layers // 2), later(x, 0)[:rows, :width], 0.0)
            ahead += jnp.where((row_at == 0) & (l >= layers // 2), earlier(x, 0)[:rows, :width], 0.0)
            ahead += later(x[:rows], 1)[:, :width]
            da, db, de = d * a, d * b, d * e
            for j, term in enumerate((da * a, da * b, db * b, db * e, de * e, e * ahead)):
                new[j] = new[j] + term
        return tuple(total + folded(x) for total, x in zip(sums, new))

    sums = list(lax.fori_loop(0, layers, moments, (jnp.zeros((8, 128), jnp.float32),) * 6))
    for c in range(3):
        joint = z2[c, H, high_half, :width] * z2[c, bottom, high_half, :width]
        for w in range(0, width, 128):
            sums[5] = sums[5] + joint[:, w : w + 128]
    sums[5] = 2.0 * sums[5]

    row = jnp.zeros((1, 128), jnp.float32)
    for j in range(6):
        row = jnp.where(tile_lane == j, jnp.sum(sums[j], keepdims=True), row)

    def exchange(value, turn, slots, count, index, peer, ssem, rsem, order):
        mine[turn] = value
        slots[index] = value
        for k in order:
            send(mine.at[turn], slots.at[index], ssem, rsem, peer(k)).start()
        return send(slots.at[pl.ds(0, count - 1)], slots.at[pl.ds(0, count - 1)], ssem, rsem, peer(1))

    def hops(k):
        across, along = k // (n_y * n_core), (k // n_core) % n_y
        return min(across, n_rad - across) + min(along, n_y - along)

    far_in_plane = sorted(range(1, n_g), key=lambda k: -hops(k))
    in_plane_copies = exchange(row, 0, plane, n_g, g, in_plane, plane_s, plane_r, far_in_plane)
    stores = [
        pltpu.make_async_copy(ref.at[:, own, pl.ds(0, rows), pl.ds(0, width)], zs_hbm.at[k], store_sem.at[k])
        for k, ref in enumerate((z0, z1, z2))
    ]
    in_plane_copies.wait_recv()
    row = jnp.sum(plane[...], axis=0)
    far_first = sorted(range(1, n_z), key=lambda k: -min(k, n_z - k))
    pl.semaphore_wait(relay, len({reach, n_z - reach}))
    copies = exchange(row, 1, column, n_z, z, along_z, column_s, column_r, far_first)

    for copy in stores:
        copy.start()
    arrived([sub_edge[0]], has_down)
    arrived([sub_edge[1]], has_up)
    arrived(rad_edge[0], has_below)
    arrived(rad_edge[1], has_above)

    def advect(l, carry):
        s = s_v[l]
        v1, v2 = motion(1, l), motion(2, l)
        total = -0.5 * s + eu0[l + 2] + ed0[l]
        u, w = (0.25 + 0.125 * v1) * s, (0.25 - 0.125 * v1) * s
        total = total + jnp.where(row_at == rows - 1, sub_in[1, layers, pl.ds(l, 1), :width], later(u, 0))
        total = total + jnp.where(row_at == 0, sub_in[0, layers, pl.ds(l, 1), :width], earlier(w, 0))
        u, w = (0.25 + 0.125 * v2) * s, (0.25 - 0.125 * v2) * s
        temp_v[l] = total + later(u, 1) + earlier(w, 1)
        return carry

    lax.fori_loop(0, layers, advect, 0)
    for l in range(layers):
        for half in range(rows // 8):
            k = l * (rows // 8) + half
            group = slice(8 * half, 8 * half + 8)
            s_low, s_high = s_v[l, group, 0:128], s_v[l, group, width - 128 : width]

            def speed(at, pick, group=group, l=l):
                return jnp.where(
                    pick == 0,
                    m_v[0, 2, l, :, at].astype(jnp.float32)[group],
                    m_v[1, 2, l, :, at].astype(jnp.float32)[group],
                )

            low, high = slice(0, 128), slice(width - 128, width)
            u = pltpu.roll((0.25 + 0.125 * speed(low, picks[0])) * s_low, 127, 1)
            w = pltpu.roll((0.25 - 0.125 * speed(high, picks[1])) * s_high, 1, 1)
            from_left = pltpu.roll(dia_in[0], (13 + 16 * k) % 128, 1)
            from_right = pltpu.roll(dia_in[1], (127 - 12 - 16 * k) % 128, 1)
            temp_v[l, group, low] += jnp.where(tile_lane == 0, from_left - w, 0.0)
            temp_v[l, group, high] += jnp.where(tile_lane == 127, from_right - u, 0.0)

    stores.append(pltpu.make_async_copy(temp_v, adv_hbm, store_sem.at[3]))
    stores[3].start()
    left_here(sub_main[0] + [sub_side[0], sub_edge[0]], has_up)
    left_here(sub_main[1] + [sub_side[1], sub_edge[1]], has_down)
    for copy in dia_copies:
        copy.wait_send()
    for group in (rad_main, rad_deep, rad_side, rad_rows, rad_edge):
        left_here(group[0], has_above)
        left_here(group[1], has_below)
    for copy in stores:
        copy.wait()
    in_plane_copies.wait_send()

    copies.wait_recv()
    copies.wait_send()
    row = jnp.sum(column[...], axis=0)
    coef_ref[...] = jnp.broadcast_to(row, (8, 128))


def finish(coef_hbm, adv_hbm, zs_hbm, temp_hbm, vel_hbm, coef, adv, zs, temp, vel, load_sem, store_sem):
    layers = adv.shape[0]
    loads, stores = [pltpu.make_async_copy(coef_hbm, coef, load_sem.at[2, 0])], []
    loads[0].start()
    for l in range(layers):
        loads.append(pltpu.make_async_copy(zs_hbm.at[:, :, l], zs.at[:, :, l], load_sem.at[0, l]))
        loads.append(pltpu.make_async_copy(adv_hbm.at[l], adv.at[l], load_sem.at[1, l]))
        stores.append(pltpu.make_async_copy(vel.at[:, l], vel_hbm.at[:, l], store_sem.at[0, l]))
        stores.append(pltpu.make_async_copy(temp.at[l], temp_hbm.at[l], store_sem.at[1, l]))
        loads[-2].start()
        loads[-1].start()
    loads[0].wait()
    row, lane = coef[0:1], lax.broadcasted_iota(jnp.int32, (1, 128), 1)
    m0, m1, m2, m3, m4, m5 = (
        jnp.sum(jnp.where(lane == j, row, 0.0), axis=1, keepdims=True) for j in range(6)
    )

    def step(p):
        a, b, c = p
        square = (a * a, 2.0 * a * b, b * b + 2.0 * a * c, 2.0 * b * c, c * c)
        energy = sum(x * m for x, m in zip(square, (m0, m1, m2, m3, m4)))
        moved = sum(x * m for x, m in zip(square, (m1, m2, m3, m4, m5)))
        return jnp.clip(energy / (energy - moved), ALPHA_LOW, ALPHA_HIGH)

    one, none = jnp.ones_like(m0), jnp.zeros_like(m0)
    p0 = (one, none, none)
    alpha0 = step(p0)
    p1 = (1.0 - alpha0, alpha0, none)
    alpha1 = step(p1)
    p2 = (p1[0] * (1.0 - alpha1), p1[1] * (1.0 - alpha1) + p1[0] * alpha1, p1[1] * alpha1)
    alpha2 = step(p2)
    c0, c1, c2 = (alpha0 * x + alpha1 * y + alpha2 * w for x, y, w in zip(p0, p1, p2))
    for l in range(layers):
        loads[2 * l + 1].wait()
        loads[2 * l + 2].wait()
        for c in range(3):
            velocity = c0 * zs[0, c, l] + c1 * zs[1, c, l] + c2 * zs[2, c, l]
            vel[c, l] = velocity
            if c == 0:
                temp[l] = adv[l] + 4.0 * velocity
        stores[2 * l].start()
        stores[2 * l + 1].start()
    for copy in stores:
        copy.wait()


def solution(mesh):
    shape = mesh.shape
    n_y = Y_COUNT if shape["sub"] >= 32 else 1
    sizes = (shape["dia"], shape["sub"], shape["rad"], n_y, CORES)
    n_z = shape["dia"] * shape["sub"] // (n_y * CORES)
    n_g = shape["rad"] * n_y * CORES

    def shards(sensitivity_heat, stored_heat, friction_diagonal, stored_motions, record_choice_table):
        layers, rows, width = sensitivity_heat.shape
        tall, wide, long = layers + 2 * H, rows + 8, width + 128
        f32 = jnp.float32
        block = pltpu.VMEM((layers, rows, width), f32)
        field = pltpu.VMEM((tall, wide, long), f32)
        vector = pltpu.VMEM((3, tall, wide, long), f32)
        dma = pltpu.SemaphoreType.DMA
        in_hbm = pl.BlockSpec(memory_space=pltpu.HBM)
        advected, zs, coefficients = pl.pallas_call(
            functools.partial(kernel, sizes),
            out_shape=(
                jax.ShapeDtypeStruct((layers, rows, width), f32),
                jax.ShapeDtypeStruct((3, 3, layers, rows, width), f32),
                jax.ShapeDtypeStruct((8, 128), f32),
            ),
            in_specs=[pl.BlockSpec(memory_space=pltpu.SMEM)] + [in_hbm] * 4,
            out_specs=(in_hbm, in_hbm, pl.BlockSpec(memory_space=pltpu.VMEM)),
            scratch_shapes=[
                block, block, pltpu.VMEM(stored_motions.shape, stored_motions.dtype),
                field, field, field, vector, vector, vector, vector,
                pltpu.VMEM((layers + 2, rows, width), f32), pltpu.VMEM((layers + 2, rows, width), f32),
                pltpu.VMEM((2, layers + 1, 8, long), f32), pltpu.VMEM((2, layers + 1, 8, long), f32),
                pltpu.VMEM((2, 8, 128), f32), pltpu.VMEM((2, 8, 128), f32),
                pltpu.VMEM((2, 2, 8, long), f32), pltpu.VMEM((2, 2, 8, long), f32),
                pltpu.VMEM((2, 8, 128), f32), pltpu.VMEM((2, 8, 128), f32), pltpu.VMEM((2, 1, 128), f32), pltpu.VMEM((n_g, 1, 128), f32), pltpu.VMEM((n_z, 1, 128), f32),
                block,
                dma((4,)), dma((4,)), dma((2,)), dma((2,)), dma((2, 2, 3)), dma((2, 2, 3)),
                dma((2, 4)), dma((2, 4)), dma((2,)), dma((2,)), dma((2, 3)), dma((2, 3)),
                dma((2, 4)), dma((2, 4)), dma((4,)), dma((4,)),
                dma, dma, dma, dma, pltpu.SemaphoreType.REGULAR,
            ],
            compiler_params=pltpu.CompilerParams(
                collective_id=0, has_side_effects=True, vmem_limit_bytes=60 * 2**20
            ),
            name="adjoint_step",
        )(record_choice_table, sensitivity_heat, stored_heat, friction_diagonal, stored_motions)
        return pl.pallas_call(
            finish,
            out_shape=(
                jax.ShapeDtypeStruct((layers, rows, width), f32),
                jax.ShapeDtypeStruct((3, layers, rows, width), f32),
            ),
            in_specs=[in_hbm] * 3,
            out_specs=(in_hbm, in_hbm),
            scratch_shapes=[
                pltpu.VMEM((8, 128), f32), block, pltpu.VMEM((3, 3, layers, rows, width), f32),
                block, pltpu.VMEM((3, layers, rows, width), f32), dma((3, layers)), dma((2, layers)),
            ],
            compiler_params=pltpu.CompilerParams(vmem_limit_bytes=60 * 2**20),
            name="finish",
        )(coefficients, advected, zs)

    placed = (
        P("rad", "sub", "dia"),
        P("rad", "sub", "dia"),
        P("rad", "sub", "dia"),
        P(None, None, "rad", "sub", "dia"),
        P("dia"),
    )
    return jax.shard_map(
        shards,
        mesh=mesh,
        in_specs=placed,
        out_specs=(P("rad", "sub", "dia"), P(None, "rad", "sub", "dia")),
        check_vma=False,
    )
```
